512 devices in a mesh: dp: 8 (over x, core), expert: 64 (over z, y).
Axes of the slice: x: 4, y: 4, z: 16, core: 2. Of those that a mesh axis runs over, the one named last changes fastest.
Arguments:
- tokens: bfloat16 [65536, 1024], P(('dp', 'expert')), may hold values from -6 to 6
- expert_ids: int32 [65536, 4], P(('dp', 'expert')), may hold values from 0 to 127, all different within a row; in each aligned block of 128 rows (0 to 127, 128 to 255, ...) at most 5 rows name the same one
- gates: bfloat16 [65536, 4], P(('dp', 'expert')), may hold values from 0.099609375 to 1
- w_up: bfloat16 [128, 1024, 512], P('expert', 'dp'), may hold values from -0.1875 to 0.1875
- w_down: bfloat16 [128, 512, 1024], P('expert', None, 'dp'), may hold values from -0.25 to 0.25
- out_grad: bfloat16 [65536, 1024], P(('dp', 'expert')), may hold values from -6 to 6
Outputs:
- mixed: bfloat16 [65536, 1024], P(('dp', 'expert'))
- tokens_grad: bfloat16 [65536, 1024], P(('dp', 'expert'))
- gate_grad: bfloat16 [65536, 4], P(('dp', 'expert'))
- up_grad: float32 [128, 1024, 512], P('expert', 'dp')
- down_grad: float32 [128, 512, 1024], P('expert', None, 'dp')
The draws below stay inside these ranges and needn't reach their ends.
Inputs may be any that keep to these rules, and one draw needn't show every extreme that they name: `expert_ids`: A token's 4 experts differ. Within the tokens of one device (aligned blocks of 128 tokens) no expert is chosen more than 5 times, and in every draw some expert is chosen exactly 5 times there; every expert is chosen somewhere.
All inputs are finite; a program needn't handle non-finite values.
Results may differ from the reference program's by a relative error of at most 0.017.
Values may be sent and summed in bfloat16 or wider, within the bound.
A program may use at most 64 MiB of HBM per device.

```python
import math
import jax
import jax.numpy as jnp
import numpy as np
from jax import lax

D = 1024
FF = 512
TOP = 4
TOK_DEV = 128
EXPERTS = 128
CAP = 5
TOKENS = 65536
N_DP = 8
N_EXPERT = 64


def level_of(rng, shape, pieces, least, top_value):
    loudness = 1.0
    for axis_at, blocks in pieces:
        draws = jax.random.uniform(jax.random.fold_in(jax.random.fold_in(rng, 6), axis_at), (blocks,), jnp.float32, least / len(pieces), top_value / len(pieces))
        loudness = loudness * jnp.repeat(jnp.exp(draws), shape[axis_at] // blocks).reshape((-1,) + (1,) * (len(shape) - 1 - axis_at))
    return loudness


def deal_out(stream_key, own, number, rows, number_of, top, reach, skew):
    ranking = jax.random.permutation(stream_key, number_of)
    packed, ordinary = portions_of(number_of, rows * top, reach, skew, True), portions_of(number_of, rows * top, reach, skew, False)
    places = jnp.arange(number_of)

    def named(sizes, offset_by):
        used = int((sizes > 0).sum())
        fixed = max(1, used // 4)
        moved = fixed + (places - fixed + offset_by * (used - fixed)) % max(1, number_of - fixed)
        return jnp.zeros((number_of,), jnp.int32).at[ranking[jnp.where(places < fixed, places, moved)]].set(jnp.asarray(sizes, jnp.int32))

    sizes = jnp.where(number % 4 == 0, named(packed, number // 4), named(ordinary, number - number // 4 - 1))
    mixed = jax.random.permutation(jax.random.fold_in(own, 3), number_of)
    giver, sink = mixed[0:number_of // 2 * 2:2], mixed[1:number_of // 2 * 2:2]
    slack = jnp.minimum(sizes[giver] - 1, reach - sizes[sink]) // 2
    slack = jnp.where((giver == ranking[0]) | (sink == ranking[0]) | (sizes[sink] == 0), 0, jnp.maximum(slack, 0))
    moved = jax.random.randint(jax.random.fold_in(own, 4), (number_of // 2,), 0, 1 << 20) % (slack + 1)
    sizes = sizes.at[giver].add(-moved).at[sink].add(moved)
    labels = jnp.searchsorted(jnp.cumsum(sizes), jnp.arange(rows * top), side="right").astype(jnp.int32)
    listing = labels.reshape(top, rows).T
    listing = listing[jax.random.permutation(jax.random.fold_in(own, 1), rows)]
    offset_by = jax.random.randint(jax.random.fold_in(own, 2), (rows, 1), 0, top)
    return jnp.take_along_axis(listing, (jnp.arange(top)[None, :] + offset_by) % top, axis=1)


def portions_of(number_of, total, reach, slope, full):
    weights = [(1 << 20) // math.isqrt(standing ** slope) + 1 for standing in range(1, number_of + 1)]
    largest = reach if full else min(reach, max(-(-total // number_of), total * weights[0] // sum(weights)))
    least = 1 if total - largest >= number_of - 1 else 0
    holding, surplus = [largest] + [least] * (number_of - 1), total - largest - least * (number_of - 1)
    while surplus > 0:
        movable = [i for i in range(1, number_of) if holding[i] < largest] or [i for i in range(1, number_of) if holding[i] < reach]
        pool, remaining = sum([weights[i] for i in movable]), surplus
        for i in movable:
            extra = min(reach - holding[i], max(1, remaining * weights[i] // pool), surplus)
            holding[i] = holding[i] + extra
            surplus = surplus - extra
    return np.array(holding)


def gaussian(key, extent, deviation, most, pieces=(), kind=jnp.bfloat16):
    loudness = level_of(key, extent, pieces, -0.22, 0.18) if pieces else 1.0
    array = jax.random.normal(key, extent, jnp.float32) * deviation * loudness
    return jnp.minimum(jnp.maximum(array, -most), most).astype(kind)


def setup_inputs(seed: int = 0) -> dict:
    arg_keys = jax.random.split(jax.random.key(seed), 7)
    tokens = gaussian(arg_keys[0], (TOKENS, D), 1.0, 6.0, ((0, 512),))
    expert_ids_keys = jax.random.split(jax.random.fold_in(arg_keys[1], 1), TOKENS // TOK_DEV)
    expert_ids_turns = jax.random.permutation(jax.random.fold_in(arg_keys[1], 3), TOKENS // TOK_DEV)
    expert_ids = jax.vmap(lambda own, number: deal_out(jax.random.fold_in(arg_keys[1], 2), own, number, TOK_DEV, EXPERTS, TOP, CAP, 1))(expert_ids_keys, expert_ids_turns).reshape((TOKENS, TOP))
    gates = jnp.clip(jnp.exp(math.log(1.0) - 2.306499 * jax.random.uniform(arg_keys[2], (TOKENS, TOP), jnp.float32) ** level_of(arg_keys[2], (TOKENS, TOP), ((0, 512),), -0.2, 0.2)), 0.099609375, 1.0).astype(jnp.bfloat16)
    w_up = gaussian(arg_keys[3], (EXPERTS, D, FF), D ** -0.5, 0.1875, ((0, 64), (1, 8)))
    w_down = gaussian(arg_keys[4], (EXPERTS, FF, D), FF ** -0.5, 0.25, ((0, 64), (2, 8)))
    out_grad = gaussian(arg_keys[5], (TOKENS, D), 1.0, 6.0, ((0, 512),))
    return dict(tokens=tokens, expert_ids=expert_ids, gates=gates, w_up=w_up, w_down=w_down, out_grad=out_grad)


def gelu(value):
    return 0.5 * value * (1.0 + jnp.tanh(0.7978845608 * (value + 0.044715 * value * value * value)))

def reference(tokens, expert_ids, gates, w_up, w_down, out_grad):
    group = TOK_DEV * N_EXPERT
    slots = group * TOP
    rows = N_EXPERT * CAP
    ids_all = expert_ids.reshape(N_DP, slots)
    gate_all = gates.reshape(N_DP, slots)
    tok_all = tokens.reshape(N_DP, group, D)
    cot_all = out_grad.reshape(N_DP, group, D)
    lanes = jnp.arange(N_DP, dtype=jnp.int32)[:, None]

    def per_group(expert, ids_row, gate_row, tok_row, cot_row, weight_up, weight_down):
        found = jnp.nonzero(ids_row == expert, size=rows, fill_value=slots)[0].astype(jnp.int32)
        valid = found < slots
        safe = jnp.minimum(found, slots - 1).astype(jnp.int32)
        token = (safe // TOP).astype(jnp.int32)
        inputs = jnp.where(valid[:, None], tok_row[token], jnp.zeros((), jnp.bfloat16))
        cotan = jnp.where(valid[:, None], cot_row[token], jnp.zeros((), jnp.bfloat16))
        weight = jnp.where(valid, gate_row[safe], jnp.zeros((), jnp.bfloat16)).astype(jnp.float32)
        pre = jnp.dot(inputs, weight_up, preferred_element_type=jnp.float32)
        act, pullback = jax.vjp(gelu, pre)
        act_b = act.astype(jnp.bfloat16)
        outs = jnp.dot(act_b, weight_down, preferred_element_type=jnp.float32).astype(jnp.bfloat16)
        scaled = (weight[:, None] * cotan.astype(jnp.float32)).astype(jnp.bfloat16)
        act_grad = jnp.dot(scaled, weight_down.T, preferred_element_type=jnp.float32)
        pre_grad = pullback(act_grad)[0].astype(jnp.bfloat16)
        row_grad = jnp.dot(pre_grad, weight_up.T, preferred_element_type=jnp.float32).astype(jnp.bfloat16)
        part_up = jnp.dot(inputs.T, pre_grad, preferred_element_type=jnp.float32).astype(jnp.bfloat16)
        part_down = jnp.dot(act_b.T, scaled, preferred_element_type=jnp.float32).astype(jnp.bfloat16)
        mix_part = weight[:, None] * outs.astype(jnp.float32)
        gate_raw = lax.optimization_barrier(jnp.sum(cotan.astype(jnp.float32) * outs.astype(jnp.float32), axis=1)).astype(jnp.bfloat16)
        gate_part = lax.optimization_barrier(gate_raw).astype(jnp.float32)
        return (token, safe, mix_part, row_grad.astype(jnp.float32), gate_part, part_up, part_down)

    def step(carry, expert):
        mix_acc, grad_acc, gate_acc = carry
        weight_up = w_up[expert]
        weight_down = w_down[expert]
        token, safe, mix_part, row_part, gate_part, part_up, part_down = jax.vmap(per_group, in_axes=(None, 0, 0, 0, 0, None, None))(expert, ids_all, gate_all, tok_all, cot_all, weight_up, weight_down)
        mix_acc = mix_acc.at[lanes, token].add(mix_part)
        grad_acc = grad_acc.at[lanes, token].add(row_part)
        gate_acc = gate_acc.at[lanes, safe].add(gate_part)
        sums = (lax.optimization_barrier(jnp.sum(part_up.astype(jnp.float32), axis=0)), lax.optimization_barrier(jnp.sum(part_down.astype(jnp.float32), axis=0)))
        return ((mix_acc, grad_acc, gate_acc), sums)
    start = (jnp.zeros((N_DP, group, D), jnp.float32), jnp.zeros((N_DP, group, D), jnp.float32), jnp.zeros((N_DP, slots), jnp.float32))
    final, grads = lax.scan(step, start, jnp.arange(EXPERTS, dtype=jnp.int32))
    mix_acc, grad_acc, gate_acc = final
    mixed = mix_acc.reshape(TOKENS, D).astype(jnp.bfloat16)
    tokens_grad = grad_acc.reshape(TOKENS, D).astype(jnp.bfloat16)
    gate_grad = gate_acc.reshape(TOKENS, TOP).astype(jnp.bfloat16)
    return (mixed, tokens_grad, gate_grad, grads[0], grads[1])
```

```python
import jax
import jax.numpy as jnp
from jax import lax
from jax.experimental import pallas as pl
from jax.experimental.pallas import tpu as pltpu
from jax.sharding import PartitionSpec as P

NX, NY, NZ = 4, 4, 16
TOK, D, FF, TOP = 128, 1024, 512, 4
BF = jnp.bfloat16
F32 = jnp.float32
MESH_ID = pl.DeviceIdType.MESH
ANY = pl.BlockSpec(memory_space=pl.ANY)
VM = pl.BlockSpec(memory_space=pltpu.VMEM)


def slot_r(k):
    return 15 if k == 8 else 2 * k - 1


def slot_l(k):
    return 15 if k == 8 else 2 * k


def places():
    dp, ex = lax.axis_index("dp"), lax.axis_index("expert")
    x, c = lax.div(dp, 2), lax.rem(dp, 2)
    z, y = lax.div(ex, NY), lax.rem(ex, NY)
    right = (dp, lax.rem(z + 1, NZ) * NY + y)
    left = (dp, lax.rem(z + NZ - 1, NZ) * NY + y)
    sib = (x * 2 + 1 - c, ex)
    xs = [(lax.rem(x + i, NX) * 2 + c, ex) for i in range(1, NX)]
    ys = [(dp, z * NY + lax.rem(y + i, NY)) for i in range(1, NY)]
    return x, y, z, c, right, left, sib, xs, ys


def greet(partners):
    barrier = pltpu.get_barrier_semaphore()
    for p in partners:
        pl.semaphore_signal(barrier, inc=1, device_id=p, device_id_type=MESH_ID)
    pl.semaphore_wait(barrier, len(partners))


def remote(src, dst, send, recv, to):
    return pltpu.make_async_remote_copy(
        src_ref=src, dst_ref=dst, send_sem=send, recv_sem=recv, device_id=to, device_id_type=MESH_ID
    )


def ag_kernel(tok, cot, meta, wu, wd, T, M, WU, WD, zs, zr, ms, mr, cs, cr, cms, cmr, ws, wr, loc):
    x, y, z, c, right, left, sib, xs, ys = places()
    greet([right, left, sib] + xs + ys)
    own = (tok, cot)
    steps = {}

    def zsend(d, k, h):
        slot = slot_r if d == 0 else slot_l
        src = own[h] if k == 1 else T.at[0, slot(k - 1), h]
        r = remote(src, T.at[0, slot(k), h], zs.at[d, k - 1, h], zr.at[d, k - 1, h], right if d == 0 else left)
        r.start()
        steps[d, k, h] = r

    def msend(d, k):
        slot = slot_r if d == 0 else slot_l
        src = meta if k == 1 else M.at[0, slot(k - 1)]
        r = remote(src, M.at[0, slot(k)], ms.at[d, k - 1], mr.at[d, k - 1], right if d == 0 else left)
        r.start()
        steps[d, k, 2] = r

    for h in (0, 1):
        for d in (0, 1):
            zsend(d, 1, h)
    for d in (0, 1):
        msend(d, 1)
    rows1 = pl.ds(pl.multiple_of(x * 256 + c * 128, 128), 128)
    rows2 = pl.ds(pl.multiple_of(x * 256, 256), 256)
    wl = [
        pltpu.make_async_copy(wu.at[c], WU.at[y, rows1], loc.at[0]),
        pltpu.make_async_copy(wd.at[c], WD.at[y, :, rows1], loc.at[1]),
    ]
    wc = [
        remote(wu.at[1 - c], WU.at[y, rows1], ws.at[0], wr.at[0], sib),
        remote(wd.at[1 - c], WD.at[y, :, rows1], ws.at[1], wr.at[1], sib),
    ]
    for r in wl + wc:
        r.start()
    own_local = [
        pltpu.make_async_copy(tok, T.at[0, 0, 0], loc.at[2]),
        pltpu.make_async_copy(cot, T.at[0, 0, 1], loc.at[3]),
        pltpu.make_async_copy(meta, M.at[0, 0], loc.at[4]),
    ]
    for r in own_local:
        r.start()
    core = [
        remote(tok, T.at[1, 0, 0], cs.at[9], cr.at[9], sib),
        remote(cot, T.at[1, 0, 1], cs.at[0], cr.at[0], sib),
        remote(meta, M.at[1, 0], cms.at[0], cmr.at[0], sib),
    ]
    for r in core:
        r.start()
    for r in wl:
        r.wait()
    for r in wc:
        r.wait_recv()
    w1 = [remote(WU.at[y, rows2], WU.at[y, rows2], ws.at[2 + i], wr.at[2 + i], xs[i]) for i in range(3)]
    w1 += [remote(WD.at[y, :, rows2], WD.at[y, :, rows2], ws.at[5 + i], wr.at[5 + i], ys[i]) for i in range(3)]
    for r in w1:
        r.start()
    w2 = [remote(WU.at[y], WU.at[y], ws.at[8 + i], wr.at[8 + i], ys[i]) for i in range(3)]
    w2 += [remote(WD.at[:, :, rows2], WD.at[:, :, rows2], ws.at[11 + i], wr.at[11 + i], xs[i]) for i in range(3)]

    for k in range(1, 9):
        for h in (0, 1):
            for d in (0, 1):
                if (d, k, h) not in steps:
                    continue
                steps[d, k, h].wait_recv()
                if k < 7 or (k == 7 and h == d):
                    zsend(d, k + 1, h)
        for d in (0, 1):
            if (d, k, 2) not in steps:
                continue
            steps[d, k, 2].wait_recv()
            if k < 7 or (k == 7 and d == 0):
                msend(d, k + 1)
        many = pl.ds(15, 1) if k == 8 else pl.ds(2 * k - 1, 2)
        pair = [
            remote(T.at[0, many], T.at[1, many], cs.at[k], cr.at[k], sib),
            remote(M.at[0, many], M.at[1, many], cms.at[k], cmr.at[k], sib),
        ]
        for r in pair:
            r.start()
        core += pair
        if k == 2:
            for r in w1:
                r.wait_recv()
            for r in w2:
                r.start()
    for r in own_local:
        r.wait()
    for r in w2 + core:
        r.wait_recv()
    for r in list(steps.values()) + wc + w1 + w2 + core:
        r.wait_send()


def codes(m, base, h):
    m = m.astype(F32)
    ids = m[0:4].astype(jnp.int32) - base
    rank = m[4:8].astype(jnp.int32)
    return jnp.where((ids & 1) == 0, ids * 8 + h * 8 + rank, -1), m[8:12]


def mid_kernel(base_ref, T, M, WU, WD, U, GP, PU, PD, X, C, G, O, R, S):
    i = pl.program_id(0)
    base = base_ref[0]

    def selection(pair):
        hot, weight, eqs = [], [], []
        for h in (0, 1):
            code, gate = codes(M[lax.div(pair, 8), lax.rem(pair, 8) * 2 + h], base, h)
            r = lax.broadcasted_iota(jnp.int32, (64, TOK), 0)
            eq = [r == code[k : k + 1] for k in range(TOP)]
            hot.append(sum(jnp.where(e, 1.0, 0.0) for e in eq))
            weight.append(sum(jnp.where(e, gate[k : k + 1], 0.0) for k, e in enumerate(eq)))
            eqs.append(eq)
        return jnp.concatenate(hot, axis=1), jnp.concatenate(weight, axis=1), eqs

    @pl.when(i < 16)
    def _():
        hot, weight, _ = selection(i)
        hot = hot.astype(BF)
        tok = jnp.dot(hot, T[0, :, 0].reshape(2 * TOK, D), preferred_element_type=F32).astype(BF)
        cot = jnp.dot(hot, T[0, :, 1].reshape(2 * TOK, D), preferred_element_type=F32).astype(BF)
        gate = jnp.broadcast_to(jnp.sum(weight, axis=1, keepdims=True), (64, 128))
        rows = pl.ds(pl.multiple_of(i * 16, 16), 16)
        for e in range(4):
            X[e, rows] = tok[e * 16 : e * 16 + 16]
            C[e, rows] = cot[e * 16 : e * 16 + 16]
            G[e, rows] = gate[e * 16 : e * 16 + 16]

    @pl.when((i >= 16) & (i < 20))
    def _():
        e = i - 16
        x, cot, wu, wd = X[e], C[e], WU[0], WD[0]
        pre = jnp.dot(x, wu, preferred_element_type=F32)
        t = jnp.tanh(0.7978845608 * (pre + 0.044715 * pre * pre * pre))
        act = (0.5 * pre * (1.0 + t)).astype(BF)
        slope = 0.5 * (1.0 + t) + 0.5 * pre * (1.0 - t * t) * (0.7978845608 * (1.0 + 0.134145 * pre * pre))
        outs = jnp.dot(act, wd, preferred_element_type=F32).astype(BF)
        O[e] = outs
        S[e] = jnp.broadcast_to(
            jnp.sum(cot.astype(F32) * outs.astype(F32), axis=1, keepdims=True), (256, 128)
        )
        scaled = (G[e][:, 0:1] * cot.astype(F32)).astype(BF)
        act_grad = lax.dot_general(scaled, wd, (((1,), (1,)), ((), ())), preferred_element_type=F32)
        pre_grad = (act_grad * slope).astype(BF)
        R[e] = lax.dot_general(pre_grad, wu, (((1,), (1,)), ((), ())), preferred_element_type=F32).astype(BF)
        PU[0] = lax.dot_general(x, pre_grad, (((0,), (0,)), ((), ())), preferred_element_type=F32).astype(BF)
        PD[0] = lax.dot_general(act, scaled, (((0,), (0,)), ((), ())), preferred_element_type=F32).astype(BF)

    @pl.when(i >= 20)
    def _():
        pair = i - 20
        hot, weight, eqs = selection(pair)
        rows = pl.ds(pl.multiple_of(pair * 16, 16), 16)
        outs = jnp.concatenate([O[e, rows] for e in range(4)], axis=0)
        grad = jnp.concatenate([R[e, rows] for e in range(4)], axis=0)
        dots = jnp.concatenate([S[e, rows] for e in range(4)], axis=0)
        over = (((0,), (0,)), ((), ()))
        mixed = lax.dot_general(weight.astype(BF), outs, over, preferred_element_type=F32).astype(BF)
        back = lax.dot_general(hot.astype(BF), grad, over, preferred_element_type=F32).astype(BF)
        for h in (0, 1):
            U[0, h, 0] = mixed[h * TOK : (h + 1) * TOK]
            U[0, h, 1] = back[h * TOK : (h + 1) * TOK]
            gp = [jnp.sum(jnp.where(eq, dots, 0.0), axis=0, keepdims=True) for eq in eqs[h]]
            gp = jnp.concatenate(gp + [jnp.zeros((12, TOK), F32)], axis=0)
            GP[lax.div(pair, 8), lax.rem(pair, 8) * 2 + h] = gp.astype(BF)


def rs_kernel(
    U, GP, PU, PD, mixed, back, gate, upg, dng,
    A, C, V, GA, GC, GV, RU, OU, SU, RU2, SU2, RU3, RD, OD, SD, RD2, SD2, RD3,
    zs, zr, ms, mr, cs, cr, cms, cmr, ws, wr, loc,
):
    x, y, z, c, right, left, sib, xs, ys = places()
    greet([right, left, sib] + xs + ys)
    groups = [pl.ds(15, 1)] + [pl.ds(2 * k - 1, 2) for k in range(7, 0, -1)] + [pl.ds(0, 1)]
    core, here = [], []
    for n, g in enumerate(groups):
        core.append(
            (
                remote(U.at[1, g], C.at[g], cs.at[n], cr.at[n], sib),
                remote(GP.at[1, g], GC.at[g], cms.at[n], cmr.at[n], sib),
            )
        )
        here.append(
            (
                pltpu.make_async_copy(U.at[0, g], A.at[g], loc.at[n]),
                pltpu.make_async_copy(GP.at[0, g], GA.at[g], loc.at[9 + n]),
            )
        )
        for r in core[n] + here[n]:
            r.start()
    xcols = [pl.ds(pl.multiple_of(lax.rem(x + i, NX) * 256, 256), 256) for i in range(NX)]
    yat = [lax.rem(y + i, NY) for i in range(NY)]
    w1 = [remote(PU.at[yat[i + 1]], RU.at[i], ws.at[i], wr.at[i], ys[i]) for i in range(3)]
    w1 += [remote(PD.at[:, :, xcols[i + 1]], RD.at[i], ws.at[3 + i], wr.at[3 + i], xs[i]) for i in range(3)]
    wl = [
        pltpu.make_async_copy(PU.at[y], OU, loc.at[18]),
        pltpu.make_async_copy(PD.at[:, :, xcols[0]], OD, loc.at[19]),
    ]
    for r in w1 + wl:
        r.start()

    sends = []
    gots = {}

    def zsend(d, k, h):
        slot = (slot_r if d == 0 else slot_l)(k)
        r = remote(A.at[slot, h], V.at[d, k - 1, h], zs.at[d, k - 1, h], zr.at[d, k - 1, h], left if d == 0 else right)
        r.start()
        sends.append(r)
        gots[d, k - 1, h] = r

    def msend(d, k):
        slot = (slot_r if d == 0 else slot_l)(k)
        r = remote(GA.at[slot], GV.at[d, k - 1], ms.at[d, k - 1], mr.at[d, k - 1], left if d == 0 else right)
        r.start()
        sends.append(r)
        gots[d, k - 1, 2] = r

    def add(slot, h, more, dst):
        @pl.loop(0, TOK, step=32)
        def _(at):
            rows = pl.ds(pl.multiple_of(at, 32), 32)
            total = A[slot, h, rows].astype(F32) + C[slot, h, rows].astype(F32)
            for d, k in more:
                total += V[d, k, h, rows].astype(F32)
            dst[rows] = total.astype(BF)

    def add_gate(slot, more):
        total = GA[slot].astype(F32) + GC[slot].astype(F32)
        for d, k in more:
            total += GV[d, k].astype(F32)
        return total.astype(BF)

    for n, k in enumerate(range(8, 0, -1)):
        for r in here[n]:
            r.wait()
        for r in core[n]:
            r.wait_recv()
        order = [(0, 1), (1, 0), (0, 0), (1, 1)] if k == 7 else [(0, 0), (1, 1)] if k == 8 else [(0, 0), (1, 0), (0, 1), (1, 1)]
        for d, h in order:
            slot = (slot_r if d == 0 else slot_l)(k)
            more = []
            if (d, k, h) in gots:
                gots[d, k, h].wait_recv()
                more = [(d, k)]
            add(slot, h, more, A.at[slot, h])
            zsend(d, k, h)
        for d in (0, 1) if k < 8 else (0,):
            slot = (slot_r if d == 0 else slot_l)(k)
            more = []
            if (d, k, 2) in gots:
                gots[d, k, 2].wait_recv()
                more = [(d, k)]
            GA[slot] = add_gate(slot, more)
            msend(d, k)
        if k == 4:
            for r in wl:
                r.wait()
            for r in w1:
                r.wait_recv()

            @pl.loop(0, D, step=32)
            def _(at):
                rows = pl.ds(pl.multiple_of(at, 32), 32)
                total = OU[rows].astype(F32)
                for i in range(3):
                    total += RU[i, rows].astype(F32)
                SU[rows] = total.astype(BF)

            @pl.loop(0, NY)
            def _(j):
                @pl.loop(0, FF, step=64)
                def _(at):
                    rows = pl.ds(pl.multiple_of(at, 64), 64)
                    total = OD[j, rows].astype(F32)
                    for i in range(3):
                        total += RD[i, j, rows].astype(F32)
                    SD[j, rows] = total.astype(BF)

            w2 = [remote(SU.at[xcols[i + 1]], RU2.at[i], ws.at[6 + i], wr.at[6 + i], xs[i]) for i in range(3)]
            w2 += [remote(SD.at[yat[i + 1]], RD2.at[i], ws.at[9 + i], wr.at[9 + i], ys[i]) for i in range(3)]
            for r in w2:
                r.start()
        if k == 2:
            for r in w2:
                r.wait_recv()

            @pl.loop(0, 256, step=32)
            def _(at):
                rows = pl.ds(pl.multiple_of(at, 32), 32)
                total = SU[pl.ds(pl.multiple_of(x * 256 + at, 32), 32)].astype(F32)
                for i in range(3):
                    total += RU2[i, rows].astype(F32)
                SU2[rows] = total.astype(BF)

            @pl.loop(0, FF, step=64)
            def _(at):
                rows = pl.ds(pl.multiple_of(at, 64), 64)
                total = SD[y, rows].astype(F32)
                for i in range(3):
                    total += RD2[i, rows].astype(F32)
                SD2[rows] = total.astype(BF)

            theirs = pl.ds(pl.multiple_of((1 - c) * 128, 128), 128)
            w3 = [
                remote(SU2.at[theirs], RU3, ws.at[12], wr.at[12], sib),
                remote(SD2.at[:, theirs], RD3, ws.at[13], wr.at[13], sib),
            ]
            for r in w3:
                r.start()
    for r in here[8]:
        r.wait()
    for r in core[8]:
        r.wait_recv()
    for r in w3:
        r.wait_recv()
    mine = pl.ds(pl.multiple_of(c * 128, 128), 128)
    upg[c] = SU2[mine].astype(F32)
    upg[1 - c] = RU3[...].astype(F32)
    dng[c] = SD2[:, mine].astype(F32)
    dng[1 - c] = RD3[...].astype(F32)
    for h, dst in ((0, mixed), (1, back)):
        for d in (0, 1):
            gots[d, 0, h].wait_recv()
        add(0, h, [(0, 0), (1, 0)], dst)
    for d in (0, 1):
        gots[d, 0, 2].wait_recv()
    gate[...] = add_gate(0, [(0, 0), (1, 0)])
    for r in sends + w1 + w2 + w3 + [r for pair in core for r in pair]:
        r.wait_send()


def shards(tokens, expert_ids, gates, w_up, w_down, out_grad):
    dma = pltpu.SemaphoreType.DMA
    z, c = lax.axis_index("expert") // NY, lax.axis_index("dp") % 2
    experts = NZ * NY * 2
    hot = (expert_ids[:, :, None] == jnp.arange(experts, dtype=jnp.int32)).astype(F32)
    before = jnp.dot(jnp.tri(TOK, k=-1, dtype=BF), jnp.sum(hot, axis=1).astype(BF), preferred_element_type=F32)
    ranks = jnp.sum(before[:, None, :] * hot, axis=2)
    meta = jnp.concatenate(
        [expert_ids.astype(BF).T, ranks.astype(BF).T, gates.T, jnp.zeros((4, TOK), BF)], axis=0
    )
    sd = jax.ShapeDtypeStruct
    T, M, WU, WD = pl.pallas_call(
        ag_kernel,
        name="gather",
        out_shape=(
            sd((2, NZ, 2, TOK, D), BF),
            sd((2, NZ, 16, TOK), BF),
            sd((NY, D, FF), BF),
            sd((NY, FF, D), BF),
        ),
        in_specs=[ANY] * 5,
        out_specs=[ANY] * 4,
        scratch_shapes=[dma((2, 8, 2))] * 2 + [dma((2, 8))] * 2 + [dma((10,))] * 2 + [dma((9,))] * 2 + [dma((14,))] * 2 + [dma((5,))],
        compiler_params=pltpu.CompilerParams(collective_id=1, has_side_effects=True),
    )(tokens, out_grad, meta, w_up, w_down)

    base = (z * (2 * NY) + c).astype(jnp.int32).reshape(1)
    pack = lambda i: jnp.minimum(i, 15)
    expert = lambda i: jnp.clip(i - 16, 0, 3)
    unpack = lambda i: jnp.maximum(i - 20, 0)
    U, GP, PU, PD = pl.pallas_call(
        mid_kernel,
        name="experts",
        grid=(36,),
        out_shape=(
            sd((2, NZ, 2, TOK, D), BF),
            sd((2, NZ, 16, TOK), BF),
            sd((NY, D, FF), BF),
            sd((NY, FF, D), BF),
        ),
        in_specs=[
            pl.BlockSpec(memory_space=pltpu.SMEM),
            pl.BlockSpec((1, 2, 2, TOK, D), lambda i: (pack(i) // 8, pack(i) % 8, 0, 0, 0)),
            pl.BlockSpec((2, NZ, 16, TOK), lambda i: (0, 0, 0, 0)),
            pl.BlockSpec((1, D, FF), lambda i: (expert(i), 0, 0)),
            pl.BlockSpec((1, FF, D), lambda i: (expert(i), 0, 0)),
        ],
        out_specs=[
            pl.BlockSpec((1, 2, 2, TOK, D), lambda i: (unpack(i) // 8, unpack(i) % 8, 0, 0, 0)),
            pl.BlockSpec((2, NZ, 16, TOK), lambda i: (0, 0, 0, 0)),
            pl.BlockSpec((1, D, FF), lambda i: (expert(i), 0, 0)),
            pl.BlockSpec((1, FF, D), lambda i: (expert(i), 0, 0)),
        ],
        scratch_shapes=[
            pltpu.VMEM((4, 256, D), BF),
            pltpu.VMEM((4, 256, D), BF),
            pltpu.VMEM((4, 256, 128), F32),
            pltpu.VMEM((4, 256, D), BF),
            pltpu.VMEM((4, 256, D), BF),
            pltpu.VMEM((4, 256, 128), F32),
        ],
        compiler_params=pltpu.CompilerParams(vmem_limit_bytes=50 << 20, dimension_semantics=("arbitrary",)),
    )(base, T, M, WU, WD)

    vm = pltpu.VMEM
    mixed, back, gate, upg, dng = pl.pallas_call(
        rs_kernel,
        name="scatter",
        out_shape=(
            sd((TOK, D), BF),
            sd((TOK, D), BF),
            sd((16, TOK), BF),
            sd((2, D // 8, FF), F32),
            sd((2, FF, D // 8), F32),
        ),
        in_specs=[ANY] * 4,
        out_specs=[VM] * 5,
        scratch_shapes=[
            vm((NZ, 2, TOK, D), BF), vm((NZ, 2, TOK, D), BF), vm((2, 8, 2, TOK, D), BF),
            vm((NZ, 16, TOK), BF), vm((NZ, 16, TOK), BF), vm((2, 8, 16, TOK), BF),
            vm((3, D, FF), BF), vm((D, FF), BF), vm((D, FF), BF), vm((3, 256, FF), BF), vm((256, FF), BF), vm((128, FF), BF),
            vm((3, NY, FF, 256), BF), vm((NY, FF, 256), BF), vm((NY, FF, 256), BF), vm((3, FF, 256), BF), vm((FF, 256), BF), vm((FF, 128), BF),
        ] + [dma((2, 8, 2))] * 2 + [dma((2, 8))] * 2 + [dma((9,))] * 4 + [dma((14,))] * 2 + [dma((20,))],
        compiler_params=pltpu.CompilerParams(collective_id=2, has_side_effects=True, vmem_limit_bytes=56 << 20),
    )(U, GP, PU, PD)
    return mixed, back, gate[:TOP].T, upg, dng


def solution(mesh):
    rows = P(("dp", "expert"), None)
    up, down = P("expert", "dp", None), P("expert", None, "dp")
    return jax.shard_map(
        shards,
        mesh=mesh,
        in_specs=(rows, rows, rows, up, down, rows),
        out_specs=(rows, rows, rows, up, down),
        check_vma=False,
    )
```

```python
import jax
import jax.numpy as jnp
from jax import lax
from jax.experimental import pallas as pl
from jax.experimental.pallas import tpu as pltpu
from jax.sharding import PartitionSpec as P

NX, NY, NZ = 4, 4, 16
TOK, D, FF, TOP = 128, 1024, 512, 4
BF = jnp.bfloat16
F32 = jnp.float32
MESH_ID = pl.DeviceIdType.MESH
ANY = pl.BlockSpec(memory_space=pl.ANY)
VM = pl.BlockSpec(memory_space=pltpu.VMEM)


def slot_r(k):
    return 15 if k == 8 else 2 * k - 1


def slot_l(k):
    return 15 if k == 8 else 2 * k


def places():
    dp, ex = lax.axis_index("dp"), lax.axis_index("expert")
    x, c = lax.div(dp, 2), lax.rem(dp, 2)
    z, y = lax.div(ex, NY), lax.rem(ex, NY)
    right = (dp, lax.rem(z + 1, NZ) * NY + y)
    left = (dp, lax.rem(z + NZ - 1, NZ) * NY + y)
    sib = (x * 2 + 1 - c, ex)
    xs = [(lax.rem(x + i, NX) * 2 + c, ex) for i in range(1, NX)]
    ys = [(dp, z * NY + lax.rem(y + i, NY)) for i in range(1, NY)]
    return x, y, z, c, right, left, sib, xs, ys


def greet(partners):
    barrier = pltpu.get_barrier_semaphore()
    for p in partners:
        pl.semaphore_signal(barrier, inc=1, device_id=p, device_id_type=MESH_ID)
    pl.semaphore_wait(barrier, len(partners))


def remote(src, dst, send, recv, to):
    return pltpu.make_async_remote_copy(
        src_ref=src, dst_ref=dst, send_sem=send, recv_sem=recv, device_id=to, device_id_type=MESH_ID
    )


def selection(meta_a, meta_b, first, core):
    hot, weight, eqs = [], [], []
    for h, m in enumerate((meta_a, meta_b)):
        m = m.astype(F32)
        at = m[0:4].astype(jnp.int32) - first
        rank = m[4:8].astype(jnp.int32)
        row = jnp.where((at & 1) == core, 0, 64) + (at >> 1) * 16 + h * 8 + rank
        row = jnp.where((at >= 0) & (at < 8), row, -1)
        r = lax.broadcasted_iota(jnp.int32, (128, TOK), 0)
        eq = [r == row[k : k + 1] for k in range(TOP)]
        hot.append(sum(jnp.where(e, 1.0, 0.0) for e in eq))
        weight.append(sum(jnp.where(e, m[8 + k : 9 + k], 0.0) for k, e in enumerate(eq)))
        eqs.append(eq)
    return jnp.concatenate(hot, axis=1), jnp.concatenate(weight, axis=1), eqs


def pair_slots(p):
    return (0, 15) if p == 0 else (2 * p - 1, 2 * p)


def ag_kernel(
    tok, cot, ids, gates, wu, wd, X, MO, WU, WD,
    T, M, B, zs, zr, ms, mr, ps, pr, lp, ws, wr, loc,
):
    x, y, z, c, right, left, sib, xs, ys = places()
    greet([right, left, sib] + xs + ys)
    own = (tok, cot)
    steps = {}

    def zsend(d, k, h):
        slot = slot_r if d == 0 else slot_l
        src = own[h] if k == 1 else T.at[slot(k - 1), h]
        r = remote(src, T.at[slot(k), h], zs.at[d, k - 1, h], zr.at[d, k - 1, h], right if d == 0 else left)
        r.start()
        steps[d, k, h] = r

    def msend(d, k):
        slot = slot_r if d == 0 else slot_l
        src = M.at[0 if k == 1 else slot(k - 1)]
        r = remote(src, M.at[slot(k)], ms.at[d, k - 1], mr.at[d, k - 1], right if d == 0 else left)
        r.start()
        steps[d, k, 2] = r

    for h in (0, 1):
        for d in (0, 1):
            zsend(d, 1, h)
    rows1 = pl.ds(pl.multiple_of(x * 256 + c * 128, 128), 128)
    rows2 = pl.ds(pl.multiple_of(x * 256, 256), 256)
    wl = [
        pltpu.make_async_copy(wu.at[c], WU.at[y, rows1], loc.at[0]),
        pltpu.make_async_copy(wd.at[c], WD.at[y, :, rows1], loc.at[1]),
    ]
    wc = [
        remote(wu.at[1 - c], WU.at[y, rows1], ws.at[0], wr.at[0], sib),
        remote(wd.at[1 - c], WD.at[y, :, rows1], ws.at[1], wr.at[1], sib),
    ]
    own_local = [
        pltpu.make_async_copy(tok, T.at[0, 0], loc.at[2]),
        pltpu.make_async_copy(cot, T.at[0, 1], loc.at[3]),
    ]
    for r in wl + wc + own_local:
        r.start()
    e = lax.broadcasted_iota(jnp.int32, (128, TOK), 0)
    eq = [e == ids[k : k + 1] for k in range(TOP)]
    hot = sum(jnp.where(q, 1.0, 0.0) for q in eq)
    earlier = jnp.where(e < lax.broadcasted_iota(jnp.int32, (128, TOK), 1), 1.0, 0.0)
    before = jnp.dot(hot.astype(BF), earlier.astype(BF), preferred_element_type=F32)
    ranks = [jnp.sum(jnp.where(q, before, 0.0), axis=0, keepdims=True) for q in eq]
    M[0] = jnp.concatenate(
        [ids[...].astype(F32)] + ranks + [gates[...].astype(F32), jnp.zeros((4, TOK), F32)], axis=0
    ).astype(BF)
    for d in (0, 1):
        msend(d, 1)
    for r in wl:
        r.wait()
    for r in wc:
        r.wait_recv()
    w1 = [remote(WU.at[y, rows2], WU.at[y, rows2], ws.at[2 + i], wr.at[2 + i], xs[i]) for i in range(3)]
    w1 += [remote(WD.at[y, :, rows2], WD.at[y, :, rows2], ws.at[5 + i], wr.at[5 + i], ys[i]) for i in range(3)]
    for r in w1:
        r.start()
    w2 = [remote(WU.at[y], WU.at[y], ws.at[8 + i], wr.at[8 + i], ys[i]) for i in range(3)]
    w2 += [remote(WD.at[:, :, rows2], WD.at[:, :, rows2], ws.at[11 + i], wr.at[11 + i], xs[i]) for i in range(3)]

    packed = []

    def pack(p):
        a, b = pair_slots(p)
        hot, weight, _ = selection(M[a], M[b], z * 8, c)
        hot = hot.astype(BF)
        gate = jnp.sum(weight, axis=1, keepdims=True)
        t = jnp.dot(hot, jnp.concatenate([T[a, 0], T[b, 0]], axis=0), preferred_element_type=F32)
        g = jnp.dot(hot, jnp.concatenate([T[a, 1], T[b, 1]], axis=0), preferred_element_type=F32)
        for n, v in enumerate((t.astype(BF), g.astype(BF), (g * gate).astype(BF))):
            for q in range(8):
                B[p, q // 4, n, q % 4] = v[q * 16 : q * 16 + 16]
        here = pltpu.make_async_copy(B.at[p, 0], X.at[:, :, pl.ds(p * 16, 16)], lp.at[p])
        there = remote(B.at[p, 1], X.at[:, :, pl.ds(128 + p * 16, 16)], ps.at[p], pr.at[p], sib)
        here.start()
        there.start()
        packed.append((here, there))

    for k in range(1, 9):
        for h in (0, 1):
            for d in (0, 1):
                if (d, k, h) not in steps:
                    continue
                steps[d, k, h].wait_recv()
                if k < 7 or (k == 7 and h == d):
                    zsend(d, k + 1, h)
        for d in (0, 1):
            if (d, k, 2) not in steps:
                continue
            steps[d, k, 2].wait_recv()
            if k < 7 or (k == 7 and d == 0):
                msend(d, k + 1)
        if k == 1:
            for r in own_local:
                r.wait()
        if k == 2:
            for r in w1:
                r.wait_recv()
            for r in w2:
                r.start()
        pack(k % 8)
    out = pltpu.make_async_copy(M, MO, loc.at[4])
    out.start()
    for r in w2:
        r.wait_recv()
    for here, there in packed:
        here.wait()
        there.wait_recv()
    for r in list(steps.values()) + wc + w1 + w2 + [there for _, there in packed]:
        r.wait_send()
    out.wait()


def mid_kernel(X, WU, WD, O, S, PU, PD):
    x, cot, scaled, wu, wd = X[0, 0], X[1, 0], X[2, 0], WU[0], WD[0]
    pre = jnp.dot(x, wu, preferred_element_type=F32)
    t = jnp.tanh(0.7978845608 * (pre + 0.044715 * pre * pre * pre))
    act = (0.5 * pre * (1.0 + t)).astype(BF)
    slope = 0.5 * (1.0 + t) + 0.5 * pre * (1.0 - t * t) * (0.7978845608 * (1.0 + 0.134145 * pre * pre))
    act_grad = lax.dot_general(scaled, wd, (((1,), (1,)), ((), ())), preferred_element_type=F32)
    pre_grad = (act_grad * slope).astype(BF)
    outs = jnp.dot(act, wd, preferred_element_type=F32).astype(BF)
    O[0, 0] = outs
    S[0] = jnp.broadcast_to(jnp.sum(cot.astype(F32) * outs.astype(F32), axis=1, keepdims=True), (256, 128))
    O[1, 0] = lax.dot_general(pre_grad, wu, (((1,), (1,)), ((), ())), preferred_element_type=F32).astype(BF)
    PU[0] = lax.dot_general(x, pre_grad, (((0,), (0,)), ((), ())), preferred_element_type=F32).astype(BF)
    PD[0] = lax.dot_general(act, scaled, (((0,), (0,)), ((), ())), preferred_element_type=F32).astype(BF)


def rs_kernel(
    O, S, MI, PU, PD, F, GO, UG, DG,
    OL, SL, M, A, V, GA, GV, FV, GF, RU, OU, SU, RU2, SU2, RU3, RD, OD, SD, RD2, SD2, RD3,
    zs, zr, ms, mr, cs, cr, ws, wr, loc,
):
    x, y, z, c, right, left, sib, xs, ys = places()
    greet([right, left, sib] + xs + ys)
    parts = [(0, 16), (112, 16), (16, 96)]
    core, here = [], [pltpu.make_async_copy(MI, M, loc.at[0])]
    here[0].start()
    for n, (at, size) in enumerate(parts):
        a, b = pl.ds(at, size), pl.ds(128 + at, size)
        pair = [
            remote(O.at[:, :, b], OL.at[1, :, :, a], cs.at[n], cr.at[n], sib),
            remote(S.at[:, b], SL.at[1, :, a], cs.at[3 + n], cr.at[3 + n], sib),
        ]
        mine = [
            pltpu.make_async_copy(O.at[:, :, a], OL.at[0, :, :, a], loc.at[1 + n]),
            pltpu.make_async_copy(S.at[:, a], SL.at[0, :, a], loc.at[4 + n]),
        ]
        for r in pair + mine:
            r.start()
        core.append(pair)
        here += mine
    xcols = [pl.ds(pl.multiple_of(lax.rem(x + i, NX) * 256, 256), 256) for i in range(NX)]
    yat = [lax.rem(y + i, NY) for i in range(NY)]
    w1 = [remote(PU.at[yat[i + 1]], RU.at[i], ws.at[i], wr.at[i], ys[i]) for i in range(3)]
    w1 += [remote(PD.at[:, :, xcols[i + 1]], RD.at[i], ws.at[3 + i], wr.at[3 + i], xs[i]) for i in range(3)]
    wl = [
        pltpu.make_async_copy(PU.at[y], OU, loc.at[7]),
        pltpu.make_async_copy(PD.at[:, :, xcols[0]], OD, loc.at[8]),
    ]
    for r in w1 + wl:
        r.start()

    sends = []
    gots = {}

    def zsend(d, k, h):
        slot = (slot_r if d == 0 else slot_l)(k)
        r = remote(A.at[slot, h], V.at[d, k - 1, h], zs.at[d, k - 1, h], zr.at[d, k - 1, h], left if d == 0 else right)
        r.start()
        sends.append(r)
        gots[d, k - 1, h] = r

    def msend(d, k):
        slot = (slot_r if d == 0 else slot_l)(k)
        r = remote(GA.at[slot], GV.at[d, k - 1], ms.at[d, k - 1], mr.at[d, k - 1], left if d == 0 else right)
        r.start()
        sends.append(r)
        gots[d, k - 1, 2] = r

    def add(slot, h, more, dst):
        @pl.loop(0, TOK, step=32)
        def _(at):
            rows = pl.ds(pl.multiple_of(at, 32), 32)
            total = A[slot, h, rows].astype(F32)
            for d, k in more:
                total += V[d, k, h, rows].astype(F32)
            dst[rows] = total.astype(BF)

    def add_gate(slot, more):
        total = GA[slot].astype(F32)
        for d, k in more:
            total += GV[d, k].astype(F32)
        return total.astype(BF)

    def unpack(p):
        slots = pair_slots(p)
        hot, weight, eqs = selection(M[slots[0]], M[slots[1]], z * 8, c)
        rows = pl.ds(p * 16, 16)
        over = (((0,), (0,)), ((), ()))
        for n, w in enumerate((weight, hot)):
            v = jnp.concatenate([OL[q // 4, n, q % 4, rows] for q in range(8)], axis=0)
            u = lax.dot_general(w.astype(BF), v, over, preferred_element_type=F32).astype(BF)
            for h, slot in enumerate(slots):
                A[slot, n] = u[h * TOK : (h + 1) * TOK]
        dots = jnp.concatenate([SL[q // 4, q % 4, rows] for q in range(8)], axis=0)
        for h, slot in enumerate(slots):
            gp = [jnp.sum(jnp.where(eq, dots, 0.0), axis=0, keepdims=True) for eq in eqs[h]]
            GA[slot] = jnp.concatenate(gp + [jnp.zeros((12, TOK), F32)], axis=0).astype(BF)

    def landed(n):
        for r in here[1 + 2 * n : 3 + 2 * n]:
            r.wait()
        for r in core[n]:
            r.wait_recv()

    here[0].wait()
    landed(0)
    unpack(0)
    for k in range(8, 0, -1):
        order = [(0, 1), (1, 0), (0, 0), (1, 1)] if k == 7 else [(0, 0), (1, 1)] if k == 8 else [(0, 0), (1, 0), (0, 1), (1, 1)]
        for d, h in order:
            slot = (slot_r if d == 0 else slot_l)(k)
            if (d, k, h) in gots:
                gots[d, k, h].wait_recv()
                add(slot, h, [(d, k)], A.at[slot, h])
            zsend(d, k, h)
        for d in (0, 1) if k < 8 else (0,):
            slot = (slot_r if d == 0 else slot_l)(k)
            if (d, k, 2) in gots:
                gots[d, k, 2].wait_recv()
                GA[slot] = add_gate(slot, [(d, k)])
            msend(d, k)
        if k == 8:
            landed(1)
        if k == 7:
            landed(2)
        if k > 1:
            unpack(k - 1)
        if k == 4:
            for r in wl:
                r.wait()
            for r in w1:
                r.wait_recv()

            @pl.loop(0, D, step=32)
            def _(at):
                rows = pl.ds(pl.multiple_of(at, 32), 32)
                total = OU[rows].astype(F32)
                for i in range(3):
                    total += RU[i, rows].astype(F32)
                SU[rows] = total.astype(BF)

            @pl.loop(0, NY)
            def _(j):
                @pl.loop(0, FF, step=64)
                def _(at):
                    rows = pl.ds(pl.multiple_of(at, 64), 64)
                    total = OD[j, rows].astype(F32)
                    for i in range(3):
                        total += RD[i, j, rows].astype(F32)
                    SD[j, rows] = total.astype(BF)

            w2 = [remote(SU.at[xcols[i + 1]], RU2.at[i], ws.at[6 + i], wr.at[6 + i], xs[i]) for i in range(3)]
            w2 += [remote(SD.at[yat[i + 1]], RD2.at[i], ws.at[9 + i], wr.at[9 + i], ys[i]) for i in range(3)]
            for r in w2:
                r.start()
        if k == 2:
            for r in w2:
                r.wait_recv()

            @pl.loop(0, 256, step=32)
            def _(at):
                rows = pl.ds(pl.multiple_of(at, 32), 32)
                total = SU[pl.ds(pl.multiple_of(x * 256 + at, 32), 32)].astype(F32)
                for i in range(3):
                    total += RU2[i, rows].astype(F32)
                SU2[rows] = total.astype(BF)

            @pl.loop(0, FF, step=64)
            def _(at):
                rows = pl.ds(pl.multiple_of(at, 64), 64)
                total = SD[y, rows].astype(F32)
                for i in range(3):
                    total += RD2[i, rows].astype(F32)
                SD2[rows] = total.astype(BF)

            theirs = pl.ds(pl.multiple_of((1 - c) * 128, 128), 128)
            w3 = [
                remote(SU2.at[theirs], RU3, ws.at[12], wr.at[12], sib),
                remote(SD2.at[:, theirs], RD3, ws.at[13], wr.at[13], sib),
            ]
            for r in w3:
                r.start()
    for r in w3:
        r.wait_recv()
    mine = pl.ds(pl.multiple_of(c * 128, 128), 128)
    last = [
        pltpu.make_async_copy(SU2.at[mine], UG.at[c], loc.at[9]),
        pltpu.make_async_copy(RU3, UG.at[1 - c], loc.at[10]),
        pltpu.make_async_copy(SD2.at[:, mine], DG.at[c], loc.at[11]),
        pltpu.make_async_copy(RD3, DG.at[1 - c], loc.at[12]),
    ]
    for r in last:
        r.start()
    for h in (0, 1):
        for d in (0, 1):
            gots[d, 0, h].wait_recv()
        add(0, h, [(0, 0), (1, 0)], FV.at[h])
        r = pltpu.make_async_copy(FV.at[h], F.at[h], loc.at[13 + h])
        r.start()
        last.append(r)
    for d in (0, 1):
        gots[d, 0, 2].wait_recv()
    GF[...] = add_gate(0, [(0, 0), (1, 0)])
    r = pltpu.make_async_copy(GF, GO, loc.at[15])
    r.start()
    last.append(r)
    for r in sends + w1 + w2 + w3 + [r for pair in core for r in pair]:
        r.wait_send()
    for r in last:
        r.wait()


def out_kernel(F, G, UG, DG, mixed, back, gate, upg, dng):
    mixed[...] = F[0]
    back[...] = F[1]
    gate[...] = G[0:TOP]
    upg[...] = UG[...].astype(F32)
    dng[...] = DG[...].astype(F32)


def shards(tokens, expert_ids, gates, w_up, w_down, out_grad):
    dma = pltpu.SemaphoreType.DMA
    sd = jax.ShapeDtypeStruct
    vm = pltpu.VMEM
    X, M, WU, WD = pl.pallas_call(
        ag_kernel,
        name="gather",
        out_shape=(
            sd((3, NY, 256, D), BF),
            sd((NZ, 16, TOK), BF),
            sd((NY, D, FF), BF),
            sd((NY, FF, D), BF),
        ),
        in_specs=[ANY, ANY, VM, VM, ANY, ANY],
        out_specs=[ANY] * 4,
        scratch_shapes=[vm((NZ, 2, TOK, D), BF), vm((NZ, 16, TOK), BF), vm((8, 2, 3, NY, 16, D), BF)]
        + [dma((2, 8, 2))] * 2 + [dma((2, 8))] * 2 + [dma((8,))] * 3 + [dma((14,))] * 2 + [dma((5,))],
        compiler_params=pltpu.CompilerParams(collective_id=1, has_side_effects=True, vmem_limit_bytes=60 << 20),
    )(tokens, out_grad, expert_ids.T, gates.T, w_up, w_down)

    O, S, PU, PD = pl.pallas_call(
        mid_kernel,
        name="experts",
        grid=(NY,),
        out_shape=(
            sd((2, NY, 256, D), BF),
            sd((NY, 256, 128), F32),
            sd((NY, D, FF), BF),
            sd((NY, FF, D), BF),
        ),
        in_specs=[
            pl.BlockSpec((3, 1, 256, D), lambda i: (0, i, 0, 0)),
            pl.BlockSpec((1, D, FF), lambda i: (i, 0, 0)),
            pl.BlockSpec((1, FF, D), lambda i: (i, 0, 0)),
        ],
        out_specs=[
            pl.BlockSpec((2, 1, 256, D), lambda i: (0, i, 0, 0)),
            pl.BlockSpec((1, 256, 128), lambda i: (i, 0, 0)),
            pl.BlockSpec((1, D, FF), lambda i: (i, 0, 0)),
            pl.BlockSpec((1, FF, D), lambda i: (i, 0, 0)),
        ],
        compiler_params=pltpu.CompilerParams(vmem_limit_bytes=60 << 20, dimension_semantics=("arbitrary",)),
    )(X, WU, WD)

    parts = pl.pallas_call(
        rs_kernel,
        name="scatter",
        out_shape=(
            sd((2, TOK, D), BF),
            sd((16, TOK), BF),
            sd((2, D // 8, FF), BF),
            sd((2, FF, D // 8), BF),
        ),
        in_specs=[ANY] * 5,
        out_specs=[ANY] * 4,
        scratch_shapes=[
            vm((2, 2, NY, 128, D), BF), vm((2, NY, 128, 128), F32), vm((NZ, 16, TOK), BF),
            vm((NZ, 2, TOK, D), BF), vm((2, 8, 2, TOK, D), BF),
            vm((NZ, 16, TOK), BF), vm((2, 8, 16, TOK), BF), vm((2, TOK, D), BF), vm((16, TOK), BF),
            vm((3, D, FF), BF), vm((D, FF), BF), vm((D, FF), BF), vm((3, 256, FF), BF), vm((256, FF), BF), vm((128, FF), BF),
            vm((3, NY, FF, 256), BF), vm((NY, FF, 256), BF), vm((NY, FF, 256), BF), vm((3, FF, 256), BF), vm((FF, 256), BF), vm((FF, 128), BF),
        ] + [dma((2, 8, 2))] * 2 + [dma((2, 8))] * 2 + [dma((6,))] * 2 + [dma((14,))] * 2 + [dma((16,))],
        compiler_params=pltpu.CompilerParams(collective_id=2, has_side_effects=True, vmem_limit_bytes=60 << 20),
    )(O, S, M, PU, PD)

    mixed, back, gate, upg, dng = pl.pallas_call(
        out_kernel,
        name="outputs",
        out_shape=(
            sd((TOK, D), BF),
            sd((TOK, D), BF),
            sd((TOP, TOK), BF),
            sd((2, D // 8, FF), F32),
            sd((2, FF, D // 8), F32),
        ),
        in_specs=[VM] * 4,
        out_specs=[VM] * 5,
    )(*parts)
    return mixed, back, gate.T, upg, dng


def solution(mesh):
    rows = P(("dp", "expert"), None)
    up, down = P("expert", "dp", None), P("expert", None, "dp")
    return jax.shard_map(
        shards,
        mesh=mesh,
        in_specs=(rows, rows, rows, up, down, rows),
        out_specs=(rows, rows, rows, up, down),
        check_vma=False,
    )
```

```python
import jax
import jax.numpy as jnp
from jax import lax
from jax.experimental import pallas as pl
from jax.experimental.pallas import tpu as pltpu
from jax.sharding import PartitionSpec as P

NX, NY, NZ = 4, 4, 16
TOK, D, FF, TOP = 128, 1024, 512, 4
BF = jnp.bfloat16
F32 = jnp.float32
MESH_ID = pl.DeviceIdType.MESH
ANY = pl.BlockSpec(memory_space=pl.ANY)
VM = pl.BlockSpec(memory_space=pltpu.VMEM)


def slot_r(k):
    return 15 if k == 8 else 2 * k - 1


def slot_l(k):
    return 15 if k == 8 else 2 * k


def places():
    dp, ex = lax.axis_index("dp"), lax.axis_index("expert")
    x, c = lax.div(dp, 2), lax.rem(dp, 2)
    z, y = lax.div(ex, NY), lax.rem(ex, NY)
    right = (dp, lax.rem(z + 1, NZ) * NY + y)
    left = (dp, lax.rem(z + NZ - 1, NZ) * NY + y)
    sib = (x * 2 + 1 - c, ex)
    xs = [(lax.rem(x + i, NX) * 2 + c, ex) for i in range(1, NX)]
    ys = [(dp, z * NY + lax.rem(y + i, NY)) for i in range(1, NY)]
    return x, y, z, c, right, left, sib, xs, ys


def greet(partners):
    barrier = pltpu.get_barrier_semaphore()
    for p in partners:
        pl.semaphore_signal(barrier, inc=1, device_id=p, device_id_type=MESH_ID)
    pl.semaphore_wait(barrier, len(partners))


def remote(src, dst, send, recv, to):
    return pltpu.make_async_remote_copy(
        src_ref=src, dst_ref=dst, send_sem=send, recv_sem=recv, device_id=to, device_id_type=MESH_ID
    )


def selection(meta_a, meta_b, first, core):
    hot, weight, eqs = [], [], []
    for h, m in enumerate((meta_a, meta_b)):
        m = m.astype(F32)
        at = m[0:4].astype(jnp.int32) - first
        rank = m[4:8].astype(jnp.int32)
        row = jnp.where((at & 1) == core, 0, 64) + (at >> 1) * 16 + h * 8 + rank
        row = jnp.where((at >= 0) & (at < 8), row, -1)
        r = lax.broadcasted_iota(jnp.int32, (128, TOK), 0)
        eq = [r == row[k : k + 1] for k in range(TOP)]
        hot.append(sum(jnp.where(e, 1.0, 0.0) for e in eq))
        weight.append(sum(jnp.where(e, m[8 + k : 9 + k], 0.0) for k, e in enumerate(eq)))
        eqs.append(eq)
    return jnp.concatenate(hot, axis=1), jnp.concatenate(weight, axis=1), eqs


def pair_slots(p):
    return (0, 15) if p == 0 else (2 * p - 1, 2 * p)


PACKED = {(11, 1): 0, (12, 0): 0, (13, 0): 0, (13, 1): 8, (14, 0): 8, (14, 1): 0, (15, 0): 8, (15, 1): 8}
ROWS = {None: TOK, 0: 80, 8: 48}


def rows_of(slot, h):
    return pl.ds(0, ROWS[PACKED.get((slot, h))])


def ahead(m, z, d):
    m = m.astype(F32)
    ids, rank = m[0:4].astype(jnp.int32), m[4:8].astype(jnp.int32)
    one, two = (lax.rem(z + (n if d == 0 else NZ - n), NZ) for n in (1, 2))
    plane = ids >> 3
    row = jnp.where(plane == one, 0, jnp.where(plane == two, 40, -1000)) + (ids & 7) * 5 + rank
    r = lax.broadcasted_iota(jnp.int32, (80, TOK), 0)
    return sum(jnp.where(r == row[k : k + 1], 1.0, 0.0) for k in range(TOP)).astype(BF)


def settle(h, first, c):
    r = lax.broadcasted_iota(jnp.int32, (128, TOK), 0)
    rank = r & 7
    at = (((r >> 4) & 3) * 2 + ((r >> 6) ^ c)) * 5 + rank + first
    at = jnp.where((((r >> 3) & 1) == h) & (rank < 5), at, -1)
    return jnp.where(lax.broadcasted_iota(jnp.int32, (128, TOK), 1) == at, 1.0, 0.0)


def routes(slots, n, dense, c, gate=None):
    made = []
    for h, slot in enumerate(slots):
        kind = PACKED.get((slot, n))
        if kind is None:
            made.append(dense[:, h * TOK : (h + 1) * TOK])
        else:
            made.append(settle(h, kind, c) if gate is None else settle(h, kind, c) * gate)
    return jnp.concatenate(made, axis=1).astype(BF)


def ag_kernel(
    tok, cot, ids, gates, wu, wd, X, MO, WU, WD,
    T, M, B, Q, zs, zr, ms, mr, ps, pr, lp, ws, wr, loc,
):
    x, y, z, c, right, left, sib, xs, ys = places()
    greet([right, left, sib] + xs + ys)
    own = (tok, cot)
    steps = {}

    def zsend(d, k, h):
        slot = slot_r if d == 0 else slot_l
        kind, rows = PACKED.get((slot(k), h)), rows_of(slot(k), h)
        if kind == 0:
            past, n = slot(k - 1), 2 * d + k - 6
            Q[n] = jnp.dot(ahead(M[past], z, d), T[past, h], preferred_element_type=F32).astype(BF)
            src = Q.at[n]
        elif kind == 8:
            src = T.at[slot(k - 1), h, pl.ds(32, 48)]
        else:
            src = own[h] if k == 1 else T.at[slot(k - 1), h]
        r = remote(src, T.at[slot(k), h, rows], zs.at[d, k - 1, h], zr.at[d, k - 1, h], right if d == 0 else left)
        r.start()
        steps[d, k, h] = r

    def msend(d, k):
        slot = slot_r if d == 0 else slot_l
        src = M.at[0 if k == 1 else slot(k - 1)]
        r = remote(src, M.at[slot(k)], ms.at[d, k - 1], mr.at[d, k - 1], right if d == 0 else left)
        r.start()
        steps[d, k, 2] = r

    for h in (0, 1):
        for d in (0, 1):
            zsend(d, 1, h)
    rows1 = pl.ds(pl.multiple_of(x * 256 + c * 128, 128), 128)
    rows2 = pl.ds(pl.multiple_of(x * 256, 256), 256)
    wl = [
        pltpu.make_async_copy(wu.at[c], WU.at[y, rows1], loc.at[0]),
        pltpu.make_async_copy(wd.at[c], WD.at[y, :, rows1], loc.at[1]),
    ]
    wc = [
        remote(wu.at[1 - c], WU.at[y, rows1], ws.at[0], wr.at[0], sib),
        remote(wd.at[1 - c], WD.at[y, :, rows1], ws.at[1], wr.at[1], sib),
    ]
    own_local = [
        pltpu.make_async_copy(tok, T.at[0, 0], loc.at[2]),
        pltpu.make_async_copy(cot, T.at[0, 1], loc.at[3]),
    ]
    for r in wl + wc + own_local:
        r.start()
    e = lax.broadcasted_iota(jnp.int32, (128, TOK), 0)
    eq = [e == ids[k : k + 1] for k in range(TOP)]
    hot = sum(jnp.where(q, 1.0, 0.0) for q in eq)
    earlier = jnp.where(e < lax.broadcasted_iota(jnp.int32, (128, TOK), 1), 1.0, 0.0)
    before = jnp.dot(hot.astype(BF), earlier.astype(BF), preferred_element_type=F32)
    ranks = [jnp.sum(jnp.where(q, before, 0.0), axis=0, keepdims=True) for q in eq]
    M[0] = jnp.concatenate(
        [ids[...].astype(F32)] + ranks + [gates[...].astype(F32), jnp.zeros((4, TOK), F32)], axis=0
    ).astype(BF)
    for d in (0, 1):
        msend(d, 1)
    for (slot, h), kind in PACKED.items():
        T[slot, h, ROWS[kind] :] = jnp.zeros((TOK - ROWS[kind], D), BF)
    for r in wl:
        r.wait()
    for r in wc:
        r.wait_recv()
    w1 = [remote(WU.at[y, rows2], WU.at[y, rows2], ws.at[2 + i], wr.at[2 + i], xs[i]) for i in range(3)]
    w1 += [remote(WD.at[y, :, rows2], WD.at[y, :, rows2], ws.at[5 + i], wr.at[5 + i], ys[i]) for i in range(3)]
    for r in w1:
        r.start()
    w2 = [remote(WU.at[y], WU.at[y], ws.at[8 + i], wr.at[8 + i], ys[i]) for i in range(3)]
    w2 += [remote(WD.at[:, :, rows2], WD.at[:, :, rows2], ws.at[11 + i], wr.at[11 + i], xs[i]) for i in range(3)]

    packed = []

    def pack(p):
        a, b = pair_slots(p)
        hot, weight, _ = selection(M[a], M[b], z * 8, c)
        gate = jnp.sum(weight, axis=1, keepdims=True)
        t = jnp.dot(routes((a, b), 0, hot, c), jnp.concatenate([T[a, 0], T[b, 0]], axis=0), preferred_element_type=F32)
        g = jnp.dot(routes((a, b), 1, hot, c), jnp.concatenate([T[a, 1], T[b, 1]], axis=0), preferred_element_type=F32)
        for n, v in enumerate((t.astype(BF), g.astype(BF), (g * gate).astype(BF))):
            for q in range(8):
                B[p, q // 4, n, q % 4] = v[q * 16 : q * 16 + 16]
        here = pltpu.make_async_copy(B.at[p, 0], X.at[:, :, pl.ds(p * 16, 16)], lp.at[p])
        there = remote(B.at[p, 1], X.at[:, :, pl.ds(128 + p * 16, 16)], ps.at[p], pr.at[p], sib)
        here.start()
        there.start()
        packed.append((here, there))

    for k in range(1, 9):
        for d in (0, 1):
            if (d, k, 2) not in steps:
                continue
            steps[d, k, 2].wait_recv()
            if k < 7 or (k == 7 and d == 0):
                msend(d, k + 1)
        for h in (0, 1):
            for d in (0, 1):
                if (d, k, h) not in steps:
                    continue
                steps[d, k, h].wait_recv()
                if k < 7 or (k == 7 and h == d):
                    zsend(d, k + 1, h)
        if k == 1:
            for r in own_local:
                r.wait()
        if k == 2:
            for r in w1:
                r.wait_recv()
            for r in w2:
                r.start()
        pack(k % 8)
    out = pltpu.make_async_copy(M, MO, loc.at[4])
    out.start()
    for r in w2:
        r.wait_recv()
    for here, there in packed:
        here.wait()
        there.wait_recv()
    for r in list(steps.values()) + wc + w1 + w2 + [there for _, there in packed]:
        r.wait_send()
    out.wait()


def mid_kernel(X, WU, WD, O, S, PU, PD):
    x, cot, scaled, wu, wd = X[0, 0], X[1, 0], X[2, 0], WU[0], WD[0]
    pre = jnp.dot(x, wu, preferred_element_type=F32)
    t = jnp.tanh(0.7978845608 * (pre + 0.044715 * pre * pre * pre))
    act = (0.5 * pre * (1.0 + t)).astype(BF)
    slope = 0.5 * (1.0 + t) + 0.5 * pre * (1.0 - t * t) * (0.7978845608 * (1.0 + 0.134145 * pre * pre))
    act_grad = lax.dot_general(scaled, wd, (((1,), (1,)), ((), ())), preferred_element_type=F32)
    pre_grad = (act_grad * slope).astype(BF)
    outs = jnp.dot(act, wd, preferred_element_type=F32).astype(BF)
    O[0, 0] = outs
    S[0] = jnp.broadcast_to(jnp.sum(cot.astype(F32) * outs.astype(F32), axis=1, keepdims=True), (256, 128))
    O[1, 0] = lax.dot_general(pre_grad, wu, (((1,), (1,)), ((), ())), preferred_element_type=F32).astype(BF)
    PU[0] = lax.dot_general(x, pre_grad, (((0,), (0,)), ((), ())), preferred_element_type=F32).astype(BF)
    PD[0] = lax.dot_general(act, scaled, (((0,), (0,)), ((), ())), preferred_element_type=F32).astype(BF)


def rs_kernel(
    O, S, MI, PU, PD, F, GO, UG, DG,
    OL, SL, M, A, V, GA, GV, FV, GF, RU, OU, SU, RU2, SU2, RU3, RD, OD, SD, RD2, SD2, RD3,
    zs, zr, ms, mr, cs, cr, ws, wr, loc,
):
    x, y, z, c, right, left, sib, xs, ys = places()
    greet([right, left, sib] + xs + ys)
    parts = [(0, 16), (112, 16), (16, 96)]
    core, here = [], [pltpu.make_async_copy(MI, M, loc.at[0])]
    here[0].start()
    for n, (at, size) in enumerate(parts):
        a, b = pl.ds(at, size), pl.ds(128 + at, size)
        pair = [
            remote(O.at[:, :, b], OL.at[1, :, :, a], cs.at[n], cr.at[n], sib),
            remote(S.at[:, b], SL.at[1, :, a], cs.at[3 + n], cr.at[3 + n], sib),
        ]
        mine = [
            pltpu.make_async_copy(O.at[:, :, a], OL.at[0, :, :, a], loc.at[1 + n]),
            pltpu.make_async_copy(S.at[:, a], SL.at[0, :, a], loc.at[4 + n]),
        ]
        for r in pair + mine:
            r.start()
        core.append(pair)
        here += mine
    xcols = [pl.ds(pl.multiple_of(lax.rem(x + i, NX) * 256, 256), 256) for i in range(NX)]
    yat = [lax.rem(y + i, NY) for i in range(NY)]
    w1 = [remote(PU.at[yat[i + 1]], RU.at[i], ws.at[i], wr.at[i], ys[i]) for i in range(3)]
    w1 += [remote(PD.at[:, :, xcols[i + 1]], RD.at[i], ws.at[3 + i], wr.at[3 + i], xs[i]) for i in range(3)]
    wl = [
        pltpu.make_async_copy(PU.at[y], OU, loc.at[7]),
        pltpu.make_async_copy(PD.at[:, :, xcols[0]], OD, loc.at[8]),
    ]
    for r in w1 + wl:
        r.start()

    sends = []
    gots = {}

    def zsend(d, k, h):
        slot = (slot_r if d == 0 else slot_l)(k)
        rows = rows_of(slot, h)
        r = remote(A.at[slot, h, rows], V.at[d, k - 1, h, rows], zs.at[d, k - 1, h], zr.at[d, k - 1, h], left if d == 0 else right)
        r.start()
        sends.append(r)
        gots[d, k - 1, h] = r

    def msend(d, k):
        slot = (slot_r if d == 0 else slot_l)(k)
        r = remote(GA.at[slot], GV.at[d, k - 1], ms.at[d, k - 1], mr.at[d, k - 1], left if d == 0 else right)
        r.start()
        sends.append(r)
        gots[d, k - 1, 2] = r

    def add(slot, h, more, dst):
        @pl.loop(0, TOK, step=32)
        def _(at):
            rows = pl.ds(pl.multiple_of(at, 32), 32)
            total = A[slot, h, rows].astype(F32)
            for d, k in more:
                total += V[d, k, h, rows].astype(F32)
            dst[rows] = total.astype(BF)

    def add_gate(slot, more):
        total = GA[slot].astype(F32)
        for d, k in more:
            total += GV[d, k].astype(F32)
        return total.astype(BF)

    def unpack(p):
        slots = pair_slots(p)
        hot, weight, eqs = selection(M[slots[0]], M[slots[1]], z * 8, c)
        rows = pl.ds(p * 16, 16)
        over = (((0,), (0,)), ((), ()))
        gate = jnp.sum(weight, axis=1, keepdims=True)
        for n, w in enumerate((routes(slots, 0, weight, c, gate), routes(slots, 1, hot, c))):
            v = jnp.concatenate([OL[q // 4, n, q % 4, rows] for q in range(8)], axis=0)
            u = lax.dot_general(w, v, over, preferred_element_type=F32).astype(BF)
            for h, slot in enumerate(slots):
                A[slot, n] = u[h * TOK : (h + 1) * TOK]
        dots = jnp.concatenate([SL[q // 4, q % 4, rows] for q in range(8)], axis=0)
        for h, slot in enumerate(slots):
            gp = [jnp.sum(jnp.where(eq, dots, 0.0), axis=0, keepdims=True) for eq in eqs[h]]
            GA[slot] = jnp.concatenate(gp + [jnp.zeros((12, TOK), F32)], axis=0).astype(BF)

    def landed(n):
        for r in here[1 + 2 * n : 3 + 2 * n]:
            r.wait()
        for r in core[n]:
            r.wait_recv()

    here[0].wait()
    landed(0)
    unpack(0)
    for k in range(8, 0, -1):
        order = [(0, 1), (1, 0), (0, 0), (1, 1)] if k == 7 else [(0, 0), (1, 1)] if k == 8 else [(0, 0), (1, 0), (0, 1), (1, 1)]
        for d, h in order:
            slot = (slot_r if d == 0 else slot_l)(k)
            if (d, k, h) in gots:
                gots[d, k, h].wait_recv()
                came = PACKED.get(((slot_r if d == 0 else slot_l)(k + 1), h))
                if came is None:
                    add(slot, h, [(d, k)], A.at[slot, h])
                elif came == 8:
                    total = A[slot, h, 32:80].astype(F32) + V[d, k, h, 0:48].astype(F32)
                    A[slot, h, 32:80] = total.astype(BF)
                else:
                    hot = ahead(M[slot], z, d)
                    total = lax.dot_general(hot, V[d, k, h, 0:80], (((0,), (0,)), ((), ())), preferred_element_type=F32)
                    A[slot, h] = (total + A[slot, h].astype(F32)).astype(BF)
            zsend(d, k, h)
        for d in (0, 1) if k < 8 else (0,):
            slot = (slot_r if d == 0 else slot_l)(k)
            if (d, k, 2) in gots:
                gots[d, k, 2].wait_recv()
                GA[slot] = add_gate(slot, [(d, k)])
            msend(d, k)
        if k == 8:
            landed(1)
        if k == 7:
            landed(2)
        if k > 1:
            unpack(k - 1)
        if k == 4:
            for r in wl:
                r.wait()
            for r in w1:
                r.wait_recv()

            @pl.loop(0, D, step=32)
            def _(at):
                rows = pl.ds(pl.multiple_of(at, 32), 32)
                total = OU[rows].astype(F32)
                for i in range(3):
                    total += RU[i, rows].astype(F32)
                SU[rows] = total.astype(BF)

            @pl.loop(0, NY)
            def _(j):
                @pl.loop(0, FF, step=64)
                def _(at):
                    rows = pl.ds(pl.multiple_of(at, 64), 64)
                    total = OD[j, rows].astype(F32)
                    for i in range(3):
                        total += RD[i, j, rows].astype(F32)
                    SD[j, rows] = total.astype(BF)

            w2 = [remote(SU.at[xcols[i + 1]], RU2.at[i], ws.at[6 + i], wr.at[6 + i], xs[i]) for i in range(3)]
            w2 += [remote(SD.at[yat[i + 1]], RD2.at[i], ws.at[9 + i], wr.at[9 + i], ys[i]) for i in range(3)]
            for r in w2:
                r.start()
        if k == 2:
            for r in w2:
                r.wait_recv()

            @pl.loop(0, 256, step=32)
            def _(at):
                rows = pl.ds(pl.multiple_of(at, 32), 32)
                total = SU[pl.ds(pl.multiple_of(x * 256 + at, 32), 32)].astype(F32)
                for i in range(3):
                    total += RU2[i, rows].astype(F32)
                SU2[rows] = total.astype(BF)

            @pl.loop(0, FF, step=64)
            def _(at):
                rows = pl.ds(pl.multiple_of(at, 64), 64)
                total = SD[y, rows].astype(F32)
                for i in range(3):
                    total += RD2[i, rows].astype(F32)
                SD2[rows] = total.astype(BF)

            theirs = pl.ds(pl.multiple_of((1 - c) * 128, 128), 128)
            w3 = [
                remote(SU2.at[theirs], RU3, ws.at[12], wr.at[12], sib),
                remote(SD2.at[:, theirs], RD3, ws.at[13], wr.at[13], sib),
            ]
            for r in w3:
                r.start()
    for r in w3:
        r.wait_recv()
    mine = pl.ds(pl.multiple_of(c * 128, 128), 128)
    last = [
        pltpu.make_async_copy(SU2.at[mine], UG.at[c], loc.at[9]),
        pltpu.make_async_copy(RU3, UG.at[1 - c], loc.at[10]),
        pltpu.make_async_copy(SD2.at[:, mine], DG.at[c], loc.at[11]),
        pltpu.make_async_copy(RD3, DG.at[1 - c], loc.at[12]),
    ]
    for r in last:
        r.start()
    for h in (0, 1):
        for d in (0, 1):
            gots[d, 0, h].wait_recv()
        add(0, h, [(0, 0), (1, 0)], FV.at[h])
        r = pltpu.make_async_copy(FV.at[h], F.at[h], loc.at[13 + h])
        r.start()
        last.append(r)
    for d in (0, 1):
        gots[d, 0, 2].wait_recv()
    GF[...] = add_gate(0, [(0, 0), (1, 0)])
    r = pltpu.make_async_copy(GF, GO, loc.at[15])
    r.start()
    last.append(r)
    for r in sends + w1 + w2 + w3 + [r for pair in core for r in pair]:
        r.wait_send()
    for r in last:
        r.wait()


def out_kernel(F, G, UG, DG, mixed, back, gate, upg, dng):
    mixed[...] = F[0]
    back[...] = F[1]
    gate[...] = G[0:TOP]
    upg[...] = UG[...].astype(F32)
    dng[...] = DG[...].astype(F32)


def shards(tokens, expert_ids, gates, w_up, w_down, out_grad):
    dma = pltpu.SemaphoreType.DMA
    sd = jax.ShapeDtypeStruct
    vm = pltpu.VMEM
    X, M, WU, WD = pl.pallas_call(
        ag_kernel,
        name="gather",
        out_shape=(
            sd((3, NY, 256, D), BF),
            sd((NZ, 16, TOK), BF),
            sd((NY, D, FF), BF),
            sd((NY, FF, D), BF),
        ),
        in_specs=[ANY, ANY, VM, VM, ANY, ANY],
        out_specs=[ANY] * 4,
        scratch_shapes=[vm((NZ, 2, TOK, D), BF), vm((NZ, 16, TOK), BF), vm((8, 2, 3, NY, 16, D), BF), vm((4, 80, D), BF)]
        + [dma((2, 8, 2))] * 2 + [dma((2, 8))] * 2 + [dma((8,))] * 3 + [dma((14,))] * 2 + [dma((5,))],
        compiler_params=pltpu.CompilerParams(collective_id=1, has_side_effects=True, vmem_limit_bytes=60 << 20),
    )(tokens, out_grad, expert_ids.T, gates.T, w_up, w_down)

    O, S, PU, PD = pl.pallas_call(
        mid_kernel,
        name="experts",
        grid=(NY,),
        out_shape=(
            sd((2, NY, 256, D), BF),
            sd((NY, 256, 128), F32),
            sd((NY, D, FF), BF),
            sd((NY, FF, D), BF),
        ),
        in_specs=[
            pl.BlockSpec((3, 1, 256, D), lambda i: (0, i, 0, 0)),
            pl.BlockSpec((1, D, FF), lambda i: (i, 0, 0)),
            pl.BlockSpec((1, FF, D), lambda i: (i, 0, 0)),
        ],
        out_specs=[
            pl.BlockSpec((2, 1, 256, D), lambda i: (0, i, 0, 0)),
            pl.BlockSpec((1, 256, 128), lambda i: (i, 0, 0)),
            pl.BlockSpec((1, D, FF), lambda i: (i, 0, 0)),
            pl.BlockSpec((1, FF, D), lambda i: (i, 0, 0)),
        ],
        compiler_params=pltpu.CompilerParams(vmem_limit_bytes=60 << 20, dimension_semantics=("arbitrary",)),
    )(X, WU, WD)

    parts = pl.pallas_call(
        rs_kernel,
        name="scatter",
        out_shape=(
            sd((2, TOK, D), BF),
            sd((16, TOK), BF),
            sd((2, D // 8, FF), BF),
            sd((2, FF, D // 8), BF),
        ),
        in_specs=[ANY] * 5,
        out_specs=[ANY] * 4,
        scratch_shapes=[
            vm((2, 2, NY, 128, D), BF), vm((2, NY, 128, 128), F32), vm((NZ, 16, TOK), BF),
            vm((NZ, 2, TOK, D), BF), vm((2, 8, 2, TOK, D), BF),
            vm((NZ, 16, TOK), BF), vm((2, 8, 16, TOK), BF), vm((2, TOK, D), BF), vm((16, TOK), BF),
            vm((3, D, FF), BF), vm((D, FF), BF), vm((D, FF), BF), vm((3, 256, FF), BF), vm((256, FF), BF), vm((128, FF), BF),
            vm((3, NY, FF, 256), BF), vm((NY, FF, 256), BF), vm((NY, FF, 256), BF), vm((3, FF, 256), BF), vm((FF, 256), BF), vm((FF, 128), BF),
        ] + [dma((2, 8, 2))] * 2 + [dma((2, 8))] * 2 + [dma((6,))] * 2 + [dma((14,))] * 2 + [dma((16,))],
        compiler_params=pltpu.CompilerParams(collective_id=2, has_side_effects=True, vmem_limit_bytes=60 << 20),
    )(O, S, M, PU, PD)

    mixed, back, gate, upg, dng = pl.pallas_call(
        out_kernel,
        name="outputs",
        out_shape=(
            sd((TOK, D), BF),
            sd((TOK, D), BF),
            sd((TOP, TOK), BF),
            sd((2, D // 8, FF), F32),
            sd((2, FF, D // 8), F32),
        ),
        in_specs=[VM] * 4,
        out_specs=[VM] * 5,
    )(*parts)
    return mixed, back, gate.T, upg, dng


def solution(mesh):
    rows = P(("dp", "expert"), None)
    up, down = P("expert", "dp", None), P("expert", None, "dp")
    return jax.shard_map(
        shards,
        mesh=mesh,
        in_specs=(rows, rows, rows, up, down, rows),
        out_specs=(rows, rows, rows, up, down),
        check_vma=False,
    )
```

```python
import jax
import jax.numpy as jnp
from jax import lax
from jax.experimental import pallas as pl
from jax.experimental.pallas import tpu as pltpu
from jax.sharding import PartitionSpec as P

NX, NY, NZ = 4, 4, 16
TOK, D, FF, TOP = 128, 1024, 512, 4
BF = jnp.bfloat16
F32 = jnp.float32
MESH_ID = pl.DeviceIdType.MESH
ANY = pl.BlockSpec(memory_space=pl.ANY)
VM = pl.BlockSpec(memory_space=pltpu.VMEM)


def slot_r(k):
    return 15 if k == 8 else 2 * k - 1


def slot_l(k):
    return 15 if k == 8 else 2 * k


def places():
    dp, ex = lax.axis_index("dp"), lax.axis_index("expert")
    x, c = lax.div(dp, 2), lax.rem(dp, 2)
    z, y = lax.div(ex, NY), lax.rem(ex, NY)
    right = (dp, lax.rem(z + 1, NZ) * NY + y)
    left = (dp, lax.rem(z + NZ - 1, NZ) * NY + y)
    sib = (x * 2 + 1 - c, ex)
    xs = [(lax.rem(x + i, NX) * 2 + c, ex) for i in range(1, NX)]
    ys = [(dp, z * NY + lax.rem(y + i, NY)) for i in range(1, NY)]
    return x, y, z, c, right, left, sib, xs, ys


def greet(partners):
    barrier = pltpu.get_barrier_semaphore()
    for p in partners:
        pl.semaphore_signal(barrier, inc=1, device_id=p, device_id_type=MESH_ID)
    pl.semaphore_wait(barrier, len(partners))


def remote(src, dst, send, recv, to):
    return pltpu.make_async_remote_copy(
        src_ref=src, dst_ref=dst, send_sem=send, recv_sem=recv, device_id=to, device_id_type=MESH_ID
    )


def selection(meta_a, meta_b, first, core):
    hot, weight, eqs = [], [], []
    for h, m in enumerate((meta_a, meta_b)):
        m = m.astype(F32)
        at = m[0:4].astype(jnp.int32) - first
        rank = m[4:8].astype(jnp.int32)
        row = jnp.where((at & 1) == core, 0, 64) + (at >> 1) * 16 + h * 8 + rank
        row = jnp.where((at >= 0) & (at < 8), row, -1)
        r = lax.broadcasted_iota(jnp.int32, (128, TOK), 0)
        eq = [r == row[k : k + 1] for k in range(TOP)]
        hot.append(sum(jnp.where(e, 1.0, 0.0) for e in eq))
        weight.append(sum(jnp.where(e, m[8 + k : 9 + k], 0.0) for k, e in enumerate(eq)))
        eqs.append(eq)
    return jnp.concatenate(hot, axis=1), jnp.concatenate(weight, axis=1), eqs


def pair_slots(p):
    return (0, 15) if p == 0 else (2 * p - 1, 2 * p)


PACKED = {(11, 1): 0, (12, 0): 0, (13, 0): 0, (13, 1): 8, (14, 0): 8, (14, 1): 0, (15, 0): 8, (15, 1): 8}
ROWS = {None: TOK, 0: 80, 8: 48}


def rows_of(slot, h):
    return pl.ds(0, ROWS[PACKED.get((slot, h))])


def ahead(m, z, d):
    m = m.astype(F32)
    ids, rank = m[0:4].astype(jnp.int32), m[4:8].astype(jnp.int32)
    one, two = (lax.rem(z + (n if d == 0 else NZ - n), NZ) for n in (1, 2))
    plane = ids >> 3
    row = jnp.where(plane == one, 0, jnp.where(plane == two, 40, -1000)) + (ids & 7) * 5 + rank
    r = lax.broadcasted_iota(jnp.int32, (80, TOK), 0)
    return sum(jnp.where(r == row[k : k + 1], 1.0, 0.0) for k in range(TOP)).astype(BF)


def settle(h, first, c):
    r = lax.broadcasted_iota(jnp.int32, (128, TOK), 0)
    rank = r & 7
    at = (((r >> 4) & 3) * 2 + ((r >> 6) ^ c)) * 5 + rank + first
    at = jnp.where((((r >> 3) & 1) == h) & (rank < 5), at, -1)
    return jnp.where(lax.broadcasted_iota(jnp.int32, (128, TOK), 1) == at, 1.0, 0.0)


def routes(slots, n, dense, c, gate=None):
    made = []
    for h, slot in enumerate(slots):
        kind = PACKED.get((slot, n))
        if kind is None:
            made.append(dense[:, h * TOK : (h + 1) * TOK])
        else:
            made.append(settle(h, kind, c) if gate is None else settle(h, kind, c) * gate)
    return jnp.concatenate(made, axis=1).astype(BF)


def ag_kernel(
    tok, cot, ids, gates, wu, wd, X, MO, WU, WD,
    T, M, B, Q, zs, zr, ms, mr, ps, pr, lp, ws, wr, loc,
):
    x, y, z, c, right, left, sib, xs, ys = places()
    greet([right, left, sib] + xs + ys)
    own = (tok, cot)
    steps = {}

    def zsend(d, k, h):
        slot = slot_r if d == 0 else slot_l
        kind, rows = PACKED.get((slot(k), h)), rows_of(slot(k), h)
        if kind == 0:
            past, n = slot(k - 1), 2 * d + k - 6
            Q[n] = jnp.dot(ahead(M[past], z, d), T[past, h], preferred_element_type=F32).astype(BF)
            src = Q.at[n]
        elif kind == 8:
            src = T.at[slot(k - 1), h, pl.ds(32, 48)]
        else:
            src = own[h] if k == 1 else T.at[slot(k - 1), h]
        r = remote(src, T.at[slot(k), h, rows], zs.at[d, k - 1, h], zr.at[d, k - 1, h], right if d == 0 else left)
        r.start()
        steps[d, k, h] = r

    def msend(d, k):
        slot = slot_r if d == 0 else slot_l
        src = M.at[0 if k == 1 else slot(k - 1)]
        r = remote(src, M.at[slot(k)], ms.at[d, k - 1], mr.at[d, k - 1], right if d == 0 else left)
        r.start()
        steps[d, k, 2] = r

    for h in (0, 1):
        for d in (0, 1):
            zsend(d, 1, h)
    rows1 = pl.ds(pl.multiple_of(x * 256 + c * 128, 128), 128)
    rows2 = pl.ds(pl.multiple_of(x * 256, 256), 256)
    wl = [
        pltpu.make_async_copy(wu.at[c], WU.at[y, rows1], loc.at[0]),
        pltpu.make_async_copy(wd.at[c], WD.at[y, :, rows1], loc.at[1]),
    ]
    wc = [
        remote(wu.at[1 - c], WU.at[y, rows1], ws.at[0], wr.at[0], sib),
        remote(wd.at[1 - c], WD.at[y, :, rows1], ws.at[1], wr.at[1], sib),
    ]
    own_local = [
        pltpu.make_async_copy(tok, T.at[0, 0], loc.at[2]),
        pltpu.make_async_copy(cot, T.at[0, 1], loc.at[3]),
    ]
    for r in wl + wc + own_local:
        r.start()
    e = lax.broadcasted_iota(jnp.int32, (128, TOK), 0)
    eq = [e == ids[k : k + 1] for k in range(TOP)]
    hot = sum(jnp.where(q, 1.0, 0.0) for q in eq)
    earlier = jnp.where(e < lax.broadcasted_iota(jnp.int32, (128, TOK), 1), 1.0, 0.0)
    before = jnp.dot(hot.astype(BF), earlier.astype(BF), preferred_element_type=F32)
    ranks = [jnp.sum(jnp.where(q, before, 0.0), axis=0, keepdims=True) for q in eq]
    M[0] = jnp.concatenate(
        [ids[...].astype(F32)] + ranks + [gates[...].astype(F32), jnp.zeros((4, TOK), F32)], axis=0
    ).astype(BF)
    for d in (0, 1):
        msend(d, 1)
    for (slot, h), kind in PACKED.items():
        T[slot, h, ROWS[kind] :] = jnp.zeros((TOK - ROWS[kind], D), BF)
    for r in wl:
        r.wait()
    for r in wc:
        r.wait_recv()
    w1 = [remote(WU.at[y, rows2], WU.at[y, rows2], ws.at[2 + i], wr.at[2 + i], xs[i]) for i in range(3)]
    w1 += [remote(WD.at[y, :, rows2], WD.at[y, :, rows2], ws.at[5 + i], wr.at[5 + i], ys[i]) for i in range(3)]
    for r in w1:
        r.start()
    w2 = [remote(WU.at[y], WU.at[y], ws.at[8 + i], wr.at[8 + i], ys[i]) for i in range(3)]
    w2 += [remote(WD.at[:, :, rows2], WD.at[:, :, rows2], ws.at[11 + i], wr.at[11 + i], xs[i]) for i in range(3)]

    packed = []

    def pack(p):
        a, b = pair_slots(p)
        hot, weight, _ = selection(M[a], M[b], z * 8, c)
        gate = jnp.sum(weight, axis=1, keepdims=True)
        t = jnp.dot(routes((a, b), 0, hot, c), jnp.concatenate([T[a, 0], T[b, 0]], axis=0), preferred_element_type=F32)
        g = jnp.dot(routes((a, b), 1, hot, c), jnp.concatenate([T[a, 1], T[b, 1]], axis=0), preferred_element_type=F32)
        for n, v in enumerate((t.astype(BF), g.astype(BF), (g * gate).astype(BF))):
            for q in range(8):
                B[p, q // 4, n, q % 4] = v[q * 16 : q * 16 + 16]
        here = pltpu.make_async_copy(B.at[p, 0], X.at[:, :, pl.ds(p * 16, 16)], lp.at[p])
        there = remote(B.at[p, 1], X.at[:, :, pl.ds(128 + p * 16, 16)], ps.at[p], pr.at[p], sib)
        here.start()
        there.start()
        packed.append((here, there))

    for k in range(1, 9):
        for d in (0, 1):
            if (d, k, 2) not in steps:
                continue
            steps[d, k, 2].wait_recv()
            if k < 7 or (k == 7 and d == 0):
                msend(d, k + 1)
        for h in (0, 1):
            for d in (0, 1):
                if (d, k, h) not in steps:
                    continue
                steps[d, k, h].wait_recv()
                if k < 7 or (k == 7 and h == d):
                    zsend(d, k + 1, h)
        if k == 1:
            for r in own_local:
                r.wait()
        pack(k % 8)
        if k == 1:
            for r in w1:
                r.wait_recv()
            for r in w2:
                r.start()
    out = pltpu.make_async_copy(M, MO, loc.at[4])
    out.start()
    for r in w2:
        r.wait_recv()
    for here, there in packed:
        here.wait()
        there.wait_recv()
    for r in list(steps.values()) + wc + w1 + w2 + [there for _, there in packed]:
        r.wait_send()
    out.wait()


def mid_kernel(X, WU, WD, O, S, PU, PD):
    x, cot, scaled, wu, wd = X[0, 0], X[1, 0], X[2, 0], WU[0], WD[0]
    pre = jnp.dot(x, wu, preferred_element_type=F32)
    t = jnp.tanh(0.7978845608 * (pre + 0.044715 * pre * pre * pre))
    act = (0.5 * pre * (1.0 + t)).astype(BF)
    slope = 0.5 * (1.0 + t) + 0.5 * pre * (1.0 - t * t) * (0.7978845608 * (1.0 + 0.134145 * pre * pre))
    act_grad = lax.dot_general(scaled, wd, (((1,), (1,)), ((), ())), preferred_element_type=F32)
    pre_grad = (act_grad * slope).astype(BF)
    outs = jnp.dot(act, wd, preferred_element_type=F32).astype(BF)
    O[0, 0] = outs
    S[0] = jnp.broadcast_to(jnp.sum(cot.astype(F32) * outs.astype(F32), axis=1, keepdims=True), (256, 128))
    O[1, 0] = lax.dot_general(pre_grad, wu, (((1,), (1,)), ((), ())), preferred_element_type=F32).astype(BF)
    PU[0] = lax.dot_general(x, pre_grad, (((0,), (0,)), ((), ())), preferred_element_type=F32).astype(BF)
    PD[0] = lax.dot_general(act, scaled, (((0,), (0,)), ((), ())), preferred_element_type=F32).astype(BF)


def rs_kernel(
    O, S, MI, PU, PD, F, GO, UG, DG,
    OL, SL, M, A, V, GA, GV, FV, GF, RU, OU, SU, RU2, SU2, RU3, RD, OD, SD, RD2, SD2, RD3,
    zs, zr, ms, mr, cs, cr, ws, wr, loc,
):
    x, y, z, c, right, left, sib, xs, ys = places()
    greet([right, left, sib] + xs + ys)
    parts = [(0, 16), (112, 16), (16, 96)]
    core, here = [], [pltpu.make_async_copy(MI, M, loc.at[0])]
    here[0].start()
    for n, (at, size) in enumerate(parts):
        a, b = pl.ds(at, size), pl.ds(128 + at, size)
        pair = [
            remote(O.at[:, :, b], OL.at[1, :, :, a], cs.at[n], cr.at[n], sib),
            remote(S.at[:, b], SL.at[1, :, a], cs.at[3 + n], cr.at[3 + n], sib),
        ]
        mine = [
            pltpu.make_async_copy(O.at[:, :, a], OL.at[0, :, :, a], loc.at[1 + n]),
            pltpu.make_async_copy(S.at[:, a], SL.at[0, :, a], loc.at[4 + n]),
        ]
        for r in pair + mine:
            r.start()
        core.append(pair)
        here += mine
    xcols = [pl.ds(pl.multiple_of(lax.rem(x + i, NX) * 256, 256), 256) for i in range(NX)]
    yat = [lax.rem(y + i, NY) for i in range(NY)]
    w1 = [remote(PU.at[yat[i + 1]], RU.at[i], ws.at[i], wr.at[i], ys[i]) for i in range(3)]
    w1 += [remote(PD.at[:, :, xcols[i + 1]], RD.at[i], ws.at[3 + i], wr.at[3 + i], xs[i]) for i in range(3)]
    wl = [
        pltpu.make_async_copy(PU.at[y], OU, loc.at[7]),
        pltpu.make_async_copy(PD.at[:, :, xcols[0]], OD, loc.at[8]),
    ]
    for r in w1 + wl:
        r.start()

    sends = []
    gots = {}

    def zsend(d, k, h):
        slot = (slot_r if d == 0 else slot_l)(k)
        rows = rows_of(slot, h)
        r = remote(A.at[slot, h, rows], V.at[d, k - 1, h, rows], zs.at[d, k - 1, h], zr.at[d, k - 1, h], left if d == 0 else right)
        r.start()
        sends.append(r)
        gots[d, k - 1, h] = r

    def msend(d, k):
        slot = (slot_r if d == 0 else slot_l)(k)
        r = remote(GA.at[slot], GV.at[d, k - 1], ms.at[d, k - 1], mr.at[d, k - 1], left if d == 0 else right)
        r.start()
        sends.append(r)
        gots[d, k - 1, 2] = r

    def add(slot, h, more, dst):
        @pl.loop(0, TOK, step=32)
        def _(at):
            rows = pl.ds(pl.multiple_of(at, 32), 32)
            total = A[slot, h, rows].astype(F32)
            for d, k in more:
                total += V[d, k, h, rows].astype(F32)
            dst[rows] = total.astype(BF)

    def add_gate(slot, more):
        total = GA[slot].astype(F32)
        for d, k in more:
            total += GV[d, k].astype(F32)
        return total.astype(BF)

    def unpack(p):
        slots = pair_slots(p)
        hot, weight, eqs = selection(M[slots[0]], M[slots[1]], z * 8, c)
        rows = pl.ds(p * 16, 16)
        over = (((0,), (0,)), ((), ()))
        gate = jnp.sum(weight, axis=1, keepdims=True)
        for n, w in enumerate((routes(slots, 0, weight, c, gate), routes(slots, 1, hot, c))):
            v = jnp.concatenate([OL[q // 4, n, q % 4, rows] for q in range(8)], axis=0)
            u = lax.dot_general(w, v, over, preferred_element_type=F32).astype(BF)
            for h, slot in enumerate(slots):
                A[slot, n] = u[h * TOK : (h + 1) * TOK]
        dots = jnp.concatenate([SL[q // 4, q % 4, rows] for q in range(8)], axis=0)
        for h, slot in enumerate(slots):
            gp = [jnp.sum(jnp.where(eq, dots, 0.0), axis=0, keepdims=True) for eq in eqs[h]]
            GA[slot] = jnp.concatenate(gp + [jnp.zeros((12, TOK), F32)], axis=0).astype(BF)

    def landed(n):
        for r in here[1 + 2 * n : 3 + 2 * n]:
            r.wait()
        for r in core[n]:
            r.wait_recv()

    here[0].wait()
    landed(0)
    unpack(0)
    for k in range(8, 0, -1):
        order = [(0, 1), (1, 0), (0, 0), (1, 1)] if k == 7 else [(0, 0), (1, 1)] if k == 8 else [(0, 0), (1, 0), (0, 1), (1, 1)]
        for d, h in order:
            slot = (slot_r if d == 0 else slot_l)(k)
            if (d, k, h) in gots:
                gots[d, k, h].wait_recv()
                came = PACKED.get(((slot_r if d == 0 else slot_l)(k + 1), h))
                if came is None:
                    add(slot, h, [(d, k)], A.at[slot, h])
                elif came == 8:
                    total = A[slot, h, 32:80].astype(F32) + V[d, k, h, 0:48].astype(F32)
                    A[slot, h, 32:80] = total.astype(BF)
                else:
                    hot = ahead(M[slot], z, d)
                    total = lax.dot_general(hot, V[d, k, h, 0:80], (((0,), (0,)), ((), ())), preferred_element_type=F32)
                    A[slot, h] = (total + A[slot, h].astype(F32)).astype(BF)
            zsend(d, k, h)
        for d in (0, 1) if k < 8 else (0,):
            slot = (slot_r if d == 0 else slot_l)(k)
            if (d, k, 2) in gots:
                gots[d, k, 2].wait_recv()
                GA[slot] = add_gate(slot, [(d, k)])
            msend(d, k)
        if k == 8:
            landed(1)
        if k == 7:
            landed(2)
        if k > 1:
            unpack(k - 1)
        if k == 2:
            for r in wl:
                r.wait()
            for r in w1:
                r.wait_recv()

            @pl.loop(0, D, step=32)
            def _(at):
                rows = pl.ds(pl.multiple_of(at, 32), 32)
                total = OU[rows].astype(F32)
                for i in range(3):
                    total += RU[i, rows].astype(F32)
                SU[rows] = total.astype(BF)

            @pl.loop(0, NY)
            def _(j):
                @pl.loop(0, FF, step=64)
                def _(at):
                    rows = pl.ds(pl.multiple_of(at, 64), 64)
                    total = OD[j, rows].astype(F32)
                    for i in range(3):
                        total += RD[i, j, rows].astype(F32)
                    SD[j, rows] = total.astype(BF)

            w2 = [remote(SU.at[xcols[i + 1]], RU2.at[i], ws.at[6 + i], wr.at[6 + i], xs[i]) for i in range(3)]
            w2 += [remote(SD.at[yat[i + 1]], RD2.at[i], ws.at[9 + i], wr.at[9 + i], ys[i]) for i in range(3)]
            for r in w2:
                r.start()
        if k == 1:
            for r in w2:
                r.wait_recv()

            @pl.loop(0, 256, step=32)
            def _(at):
                rows = pl.ds(pl.multiple_of(at, 32), 32)
                total = SU[pl.ds(pl.multiple_of(x * 256 + at, 32), 32)].astype(F32)
                for i in range(3):
                    total += RU2[i, rows].astype(F32)
                SU2[rows] = total.astype(BF)

            @pl.loop(0, FF, step=64)
            def _(at):
                rows = pl.ds(pl.multiple_of(at, 64), 64)
                total = SD[y, rows].astype(F32)
                for i in range(3):
                    total += RD2[i, rows].astype(F32)
                SD2[rows] = total.astype(BF)

            theirs = pl.ds(pl.multiple_of((1 - c) * 128, 128), 128)
            w3 = [
                remote(SU2.at[theirs], RU3, ws.at[12], wr.at[12], sib),
                remote(SD2.at[:, theirs], RD3, ws.at[13], wr.at[13], sib),
            ]
            for r in w3:
                r.start()
    for r in w3:
        r.wait_recv()
    mine = pl.ds(pl.multiple_of(c * 128, 128), 128)
    last = [
        pltpu.make_async_copy(SU2.at[mine], UG.at[c], loc.at[9]),
        pltpu.make_async_copy(RU3, UG.at[1 - c], loc.at[10]),
        pltpu.make_async_copy(SD2.at[:, mine], DG.at[c], loc.at[11]),
        pltpu.make_async_copy(RD3, DG.at[1 - c], loc.at[12]),
    ]
    for r in last:
        r.start()
    for h in (0, 1):
        for d in (0, 1):
            gots[d, 0, h].wait_recv()
        add(0, h, [(0, 0), (1, 0)], FV.at[h])
        r = pltpu.make_async_copy(FV.at[h], F.at[h], loc.at[13 + h])
        r.start()
        last.append(r)
    for d in (0, 1):
        gots[d, 0, 2].wait_recv()
    GF[...] = add_gate(0, [(0, 0), (1, 0)])
    r = pltpu.make_async_copy(GF, GO, loc.at[15])
    r.start()
    last.append(r)
    for r in sends + w1 + w2 + w3 + [r for pair in core for r in pair]:
        r.wait_send()
    for r in last:
        r.wait()


def out_kernel(F, G, UG, DG, mixed, back, gate, upg, dng):
    mixed[...] = F[0]
    back[...] = F[1]
    gate[...] = G[0:TOP]
    upg[...] = UG[...].astype(F32)
    dng[...] = DG[...].astype(F32)


def shards(tokens, expert_ids, gates, w_up, w_down, out_grad):
    dma = pltpu.SemaphoreType.DMA
    sd = jax.ShapeDtypeStruct
    vm = pltpu.VMEM
    X, M, WU, WD = pl.pallas_call(
        ag_kernel,
        name="gather",
        out_shape=(
            sd((3, NY, 256, D), BF),
            sd((NZ, 16, TOK), BF),
            sd((NY, D, FF), BF),
            sd((NY, FF, D), BF),
        ),
        in_specs=[ANY, ANY, VM, VM, ANY, ANY],
        out_specs=[ANY] * 4,
        scratch_shapes=[vm((NZ, 2, TOK, D), BF), vm((NZ, 16, TOK), BF), vm((8, 2, 3, NY, 16, D), BF), vm((4, 80, D), BF)]
        + [dma((2, 8, 2))] * 2 + [dma((2, 8))] * 2 + [dma((8,))] * 3 + [dma((14,))] * 2 + [dma((5,))],
        compiler_params=pltpu.CompilerParams(collective_id=1, has_side_effects=True, vmem_limit_bytes=60 << 20),
    )(tokens, out_grad, expert_ids.T, gates.T, w_up, w_down)

    O, S, PU, PD = pl.pallas_call(
        mid_kernel,
        name="experts",
        grid=(NY,),
        out_shape=(
            sd((2, NY, 256, D), BF),
            sd((NY, 256, 128), F32),
            sd((NY, D, FF), BF),
            sd((NY, FF, D), BF),
        ),
        in_specs=[
            pl.BlockSpec((3, 1, 256, D), lambda i: (0, i, 0, 0)),
            pl.BlockSpec((1, D, FF), lambda i: (i, 0, 0)),
            pl.BlockSpec((1, FF, D), lambda i: (i, 0, 0)),
        ],
        out_specs=[
            pl.BlockSpec((2, 1, 256, D), lambda i: (0, i, 0, 0)),
            pl.BlockSpec((1, 256, 128), lambda i: (i, 0, 0)),
            pl.BlockSpec((1, D, FF), lambda i: (i, 0, 0)),
            pl.BlockSpec((1, FF, D), lambda i: (i, 0, 0)),
        ],
        compiler_params=pltpu.CompilerParams(vmem_limit_bytes=60 << 20, dimension_semantics=("arbitrary",)),
    )(X, WU, WD)

    parts = pl.pallas_call(
        rs_kernel,
        name="scatter",
        out_shape=(
            sd((2, TOK, D), BF),
            sd((16, TOK), BF),
            sd((2, D // 8, FF), BF),
            sd((2, FF, D // 8), BF),
        ),
        in_specs=[ANY] * 5,
        out_specs=[ANY] * 4,
        scratch_shapes=[
            vm((2, 2, NY, 128, D), BF), vm((2, NY, 128, 128), F32), vm((NZ, 16, TOK), BF),
            vm((NZ, 2, TOK, D), BF), vm((2, 8, 2, TOK, D), BF),
            vm((NZ, 16, TOK), BF), vm((2, 8, 16, TOK), BF), vm((2, TOK, D), BF), vm((16, TOK), BF),
            vm((3, D, FF), BF), vm((D, FF), BF), vm((D, FF), BF), vm((3, 256, FF), BF), vm((256, FF), BF), vm((128, FF), BF),
            vm((3, NY, FF, 256), BF), vm((NY, FF, 256), BF), vm((NY, FF, 256), BF), vm((3, FF, 256), BF), vm((FF, 256), BF), vm((FF, 128), BF),
        ] + [dma((2, 8, 2))] * 2 + [dma((2, 8))] * 2 + [dma((6,))] * 2 + [dma((14,))] * 2 + [dma((16,))],
        compiler_params=pltpu.CompilerParams(collective_id=2, has_side_effects=True, vmem_limit_bytes=60 << 20),
    )(O, S, M, PU, PD)

    mixed, back, gate, upg, dng = pl.pallas_call(
        out_kernel,
        name="outputs",
        out_shape=(
            sd((TOK, D), BF),
            sd((TOK, D), BF),
            sd((TOP, TOK), BF),
            sd((2, D // 8, FF), F32),
            sd((2, FF, D // 8), F32),
        ),
        in_specs=[VM] * 4,
        out_specs=[VM] * 5,
    )(*parts)
    return mixed, back, gate.T, upg, dng


def solution(mesh):
    rows = P(("dp", "expert"), None)
    up, down = P("expert", "dp", None), P("expert", None, "dp")
    return jax.shard_map(
        shards,
        mesh=mesh,
        in_specs=(rows, rows, rows, up, down, rows),
        out_specs=(rows, rows, rows, up, down),
        check_vma=False,
    )
```

```python
import jax
import jax.numpy as jnp
from jax import lax
from jax.experimental import pallas as pl
from jax.experimental.pallas import tpu as pltpu
from jax.sharding import PartitionSpec as P

NX, NY, NZ = 4, 4, 16
TOK, D, FF, TOP = 128, 1024, 512, 4
BF = jnp.bfloat16
F32 = jnp.float32
MESH_ID = pl.DeviceIdType.MESH
ANY = pl.BlockSpec(memory_space=pl.ANY)
VM = pl.BlockSpec(memory_space=pltpu.VMEM)


def slot_r(k):
    return 15 if k == 8 else 2 * k - 1


def slot_l(k):
    return 15 if k == 8 else 2 * k


def places():
    dp, ex = lax.axis_index("dp"), lax.axis_index("expert")
    x, c = lax.div(dp, 2), lax.rem(dp, 2)
    z, y = lax.div(ex, NY), lax.rem(ex, NY)
    right = (dp, lax.rem(z + 1, NZ) * NY + y)
    left = (dp, lax.rem(z + NZ - 1, NZ) * NY + y)
    sib = (x * 2 + 1 - c, ex)
    xs = [(lax.rem(x + i, NX) * 2 + c, ex) for i in range(1, NX)]
    ys = [(dp, z * NY + lax.rem(y + i, NY)) for i in range(1, NY)]
    return x, y, z, c, right, left, sib, xs, ys


def greet(partners):
    barrier = pltpu.get_barrier_semaphore()
    for p in partners:
        pl.semaphore_signal(barrier, inc=1, device_id=p, device_id_type=MESH_ID)
    pl.semaphore_wait(barrier, len(partners))


def remote(src, dst, send, recv, to):
    return pltpu.make_async_remote_copy(
        src_ref=src, dst_ref=dst, send_sem=send, recv_sem=recv, device_id=to, device_id_type=MESH_ID
    )


def selection(meta_a, meta_b, first, core):
    hot, weight, eqs = [], [], []
    for h, m in enumerate((meta_a, meta_b)):
        m = m.astype(F32)
        at = m[0:4].astype(jnp.int32) - first
        rank = m[4:8].astype(jnp.int32)
        row = jnp.where((at & 1) == core, 0, 64) + (at >> 1) * 16 + h * 8 + rank
        row = jnp.where((at >= 0) & (at < 8), row, -1)
        r = lax.broadcasted_iota(jnp.int32, (128, TOK), 0)
        eq = [r == row[k : k + 1] for k in range(TOP)]
        hot.append(sum(jnp.where(e, 1.0, 0.0) for e in eq))
        weight.append(sum(jnp.where(e, m[8 + k : 9 + k], 0.0) for k, e in enumerate(eq)))
        eqs.append(eq)
    return jnp.concatenate(hot, axis=1), jnp.concatenate(weight, axis=1), eqs


def pair_slots(p):
    return (0, 15) if p == 0 else (2 * p - 1, 2 * p)


PACKED = {(11, 1): 0, (12, 0): 0, (13, 0): 0, (13, 1): 8, (14, 0): 8, (14, 1): 0, (15, 0): 8, (15, 1): 8}
ROWS = {None: TOK, 0: 80, 8: 48}


def rows_of(slot, h):
    return pl.ds(0, ROWS[PACKED.get((slot, h))])


def ahead(m, z, d):
    m = m.astype(F32)
    ids, rank = m[0:4].astype(jnp.int32), m[4:8].astype(jnp.int32)
    one, two = (lax.rem(z + (n if d == 0 else NZ - n), NZ) for n in (1, 2))
    plane = ids >> 3
    row = jnp.where(plane == one, 0, jnp.where(plane == two, 40, -1000)) + (ids & 7) * 5 + rank
    r = lax.broadcasted_iota(jnp.int32, (80, TOK), 0)
    return sum(jnp.where(r == row[k : k + 1], 1.0, 0.0) for k in range(TOP)).astype(BF)


def settle(h, first, c):
    r = lax.broadcasted_iota(jnp.int32, (128, TOK), 0)
    rank = r & 7
    at = (((r >> 4) & 3) * 2 + ((r >> 6) ^ c)) * 5 + rank + first
    at = jnp.where((((r >> 3) & 1) == h) & (rank < 5), at, -1)
    return jnp.where(lax.broadcasted_iota(jnp.int32, (128, TOK), 1) == at, 1.0, 0.0)


def routes(slots, n, dense, c, gate=None):
    made = []
    for h, slot in enumerate(slots):
        kind = PACKED.get((slot, n))
        if kind is None:
            made.append(dense[:, h * TOK : (h + 1) * TOK])
        else:
            made.append(settle(h, kind, c) if gate is None else settle(h, kind, c) * gate)
    return jnp.concatenate(made, axis=1).astype(BF)


def ag_kernel(
    tok, cot, ids, gates, wu, wd, X, MO, WU, WD,
    T, M, B, Q, zs, zr, ms, mr, ps, pr, lp, ws, wr, loc,
):
    x, y, z, c, right, left, sib, xs, ys = places()
    greet([right, left, sib] + xs + ys)
    own = (tok, cot)
    steps = {}

    def zsend(d, k, h):
        slot = slot_r if d == 0 else slot_l
        kind, rows = PACKED.get((slot(k), h)), rows_of(slot(k), h)
        if kind == 0:
            past, n = slot(k - 1), 2 * d + k - 6
            Q[n] = jnp.dot(ahead(M[past], z, d), T[past, h], preferred_element_type=F32).astype(BF)
            src = Q.at[n]
        elif kind == 8:
            src = T.at[slot(k - 1), h, pl.ds(32, 48)]
        else:
            src = own[h] if k == 1 else T.at[slot(k - 1), h]
        r = remote(src, T.at[slot(k), h, rows], zs.at[d, k - 1, h], zr.at[d, k - 1, h], right if d == 0 else left)
        r.start()
        steps[d, k, h] = r

    def msend(d, k):
        slot = slot_r if d == 0 else slot_l
        src = M.at[0 if k == 1 else slot(k - 1)]
        r = remote(src, M.at[slot(k)], ms.at[d, k - 1], mr.at[d, k - 1], right if d == 0 else left)
        r.start()
        steps[d, k, 2] = r

    for h in (0, 1):
        for d in (0, 1):
            zsend(d, 1, h)
    rows1 = pl.ds(pl.multiple_of(x * 256 + c * 128, 128), 128)
    rows2 = pl.ds(pl.multiple_of(x * 256, 256), 256)
    wl = [
        pltpu.make_async_copy(wu.at[c], WU.at[y, rows1], loc.at[0]),
        pltpu.make_async_copy(wd.at[c], WD.at[y, :, rows1], loc.at[1]),
    ]
    wc = [
        remote(wu.at[1 - c], WU.at[y, rows1], ws.at[0], wr.at[0], sib),
        remote(wd.at[1 - c], WD.at[y, :, rows1], ws.at[1], wr.at[1], sib),
    ]
    own_local = [
        pltpu.make_async_copy(tok, T.at[0, 0], loc.at[2]),
        pltpu.make_async_copy(cot, T.at[0, 1], loc.at[3]),
    ]
    for r in wl + wc + own_local:
        r.start()
    e = lax.broadcasted_iota(jnp.int32, (128, TOK), 0)
    eq = [e == ids[k : k + 1] for k in range(TOP)]
    hot = sum(jnp.where(q, 1.0, 0.0) for q in eq)
    earlier = jnp.where(e < lax.broadcasted_iota(jnp.int32, (128, TOK), 1), 1.0, 0.0)
    before = jnp.dot(hot.astype(BF), earlier.astype(BF), preferred_element_type=F32)
    ranks = [jnp.sum(jnp.where(q, before, 0.0), axis=0, keepdims=True) for q in eq]
    M[0] = jnp.concatenate(
        [ids[...].astype(F32)] + ranks + [gates[...].astype(F32), jnp.zeros((4, TOK), F32)], axis=0
    ).astype(BF)
    for d in (0, 1):
        msend(d, 1)
    for (slot, h), kind in PACKED.items():
        T[slot, h, ROWS[kind] :] = jnp.zeros((TOK - ROWS[kind], D), BF)
    for r in wl:
        r.wait()
    for r in wc:
        r.wait_recv()
    w1 = [remote(WU.at[y, rows2], WU.at[y, rows2], ws.at[2 + i], wr.at[2 + i], xs[i]) for i in range(3)]
    w1 += [remote(WD.at[y, :, rows2], WD.at[y, :, rows2], ws.at[5 + i], wr.at[5 + i], ys[i]) for i in range(3)]
    for r in w1:
        r.start()
    w2 = [remote(WU.at[y], WU.at[y], ws.at[8 + i], wr.at[8 + i], ys[i]) for i in range(3)]
    w2 += [remote(WD.at[:, :, rows2], WD.at[:, :, rows2], ws.at[11 + i], wr.at[11 + i], xs[i]) for i in range(3)]

    packed = []

    def choose(p):
        a, b = pair_slots(p)
        hot, weight, _ = selection(M[a], M[b], z * 8, c)
        return routes((a, b), 0, hot, c), routes((a, b), 1, hot, c), jnp.sum(weight, axis=1, keepdims=True)

    def pack(p, chosen):
        a, b = pair_slots(p)
        for_tok, for_cot, gate = chosen
        t = jnp.dot(for_tok, jnp.concatenate([T[a, 0], T[b, 0]], axis=0), preferred_element_type=F32)
        g = jnp.dot(for_cot, jnp.concatenate([T[a, 1], T[b, 1]], axis=0), preferred_element_type=F32)
        for n, v in enumerate((t.astype(BF), g.astype(BF), (g * gate).astype(BF))):
            for q in range(8):
                B[p, q // 4, n, q % 4] = v[q * 16 : q * 16 + 16]
        here = pltpu.make_async_copy(B.at[p, 0], X.at[:, :, pl.ds(p * 16, 16)], lp.at[p])
        there = remote(B.at[p, 1], X.at[:, :, pl.ds(128 + p * 16, 16)], ps.at[p], pr.at[p], sib)
        here.start()
        there.start()
        packed.append((here, there))

    for k in range(1, 9):
        for d in (0, 1):
            if (d, k, 2) not in steps:
                continue
            steps[d, k, 2].wait_recv()
            if k < 7 or (k == 7 and d == 0):
                msend(d, k + 1)
        chosen = choose(0) if k == 8 else None
        for h in (0, 1):
            for d in (0, 1):
                if (d, k, h) not in steps:
                    continue
                steps[d, k, h].wait_recv()
                if k < 7 or (k == 7 and h == d):
                    zsend(d, k + 1, h)
        if k == 1:
            for r in own_local:
                r.wait()
        pack(k % 8, chosen or choose(k))
        if k == 1:
            for r in w1:
                r.wait_recv()
            for r in w2:
                r.start()
    out = pltpu.make_async_copy(M, MO, loc.at[4])
    out.start()
    for r in w2:
        r.wait_recv()
    for here, there in packed:
        here.wait()
        there.wait_recv()
    for r in list(steps.values()) + wc + w1 + w2 + [there for _, there in packed]:
        r.wait_send()
    out.wait()


def rs_kernel(
    X, MI, WU, WD, F, GO, UG, DG,
    XV, WUV, WDV, OB, OR, SB, SR, AC, PG, PU, PD,
    M, A, V, GA, GV, FV, GF, RU, SU, RU2, SU2, RU3, RD, OD, SD, RD2, SD2, RD3,
    zs, zr, ms, mr, cs, cr, ws, wr, loc, ld,
):
    x, y, z, c, right, left, sib, xs, ys = places()
    loads = {}

    def load(e):
        loads[e] = [
            pltpu.make_async_copy(X.at[:, e], XV.at[:, e], ld.at[e, 0]),
            pltpu.make_async_copy(WU.at[e], WUV.at[e % 2], ld.at[e, 1]),
            pltpu.make_async_copy(WD.at[e], WDV.at[e % 2], ld.at[e, 2]),
        ]
        for r in loads[e]:
            r.start()

    load(0)
    load(1)
    near = pltpu.make_async_copy(MI, M, loc.at[0])
    near.start()
    greet([right, left, sib] + xs + ys)
    core = []
    for e in range(NY):
        for r in loads[e]:
            r.wait()
        rows, cot, scaled, wu, wd = XV[0, e], XV[1, e], XV[2, e], WUV[e % 2], WDV[e % 2]
        pre = jnp.dot(rows, wu, preferred_element_type=F32)
        t = jnp.tanh(0.7978845608 * (pre + 0.044715 * pre * pre * pre))
        act = (0.5 * pre * (1.0 + t)).astype(BF)
        slope = 0.5 * (1.0 + t) + 0.5 * pre * (1.0 - t * t) * (0.7978845608 * (1.0 + 0.134145 * pre * pre))
        act_grad = lax.dot_general(scaled, wd, (((1,), (1,)), ((), ())), preferred_element_type=F32)
        pre_grad = (act_grad * slope).astype(BF)
        outs = jnp.dot(act, wd, preferred_element_type=F32).astype(BF)
        OB[0, e] = outs
        SB[e] = jnp.broadcast_to(jnp.sum(cot.astype(F32) * outs.astype(F32), axis=1, keepdims=True), (256, 128))
        OB[1, e] = lax.dot_general(pre_grad, wu, (((1,), (1,)), ((), ())), preferred_element_type=F32).astype(BF)
        AC[e] = act
        PG[e] = pre_grad
        pair = [
            remote(OB.at[:, e, pl.ds(128, 128)], OR.at[:, e], cs.at[e], cr.at[e], sib),
            remote(SB.at[e, pl.ds(128, 128)], SR.at[e], cs.at[4 + e], cr.at[4 + e], sib),
        ]
        for r in pair:
            r.start()
        core += pair
        if e < 2:
            load(e + 2)

    def weigh(e):
        over = (((0,), (0,)), ((), ()))
        PU[e] = lax.dot_general(XV[0, e], PG[e], over, preferred_element_type=F32).astype(BF)
        PD[e] = lax.dot_general(AC[e], XV[2, e], over, preferred_element_type=F32).astype(BF)

    xcols = [pl.ds(pl.multiple_of(lax.rem(x + i, NX) * 256, 256), 256) for i in range(NX)]
    yat = [lax.rem(y + i, NY) for i in range(NY)]
    w1 = [remote(PU.at[yat[i + 1]], RU.at[i], ws.at[i], wr.at[i], ys[i]) for i in range(3)]
    w1 += [remote(PD.at[:, :, xcols[i + 1]], RD.at[i], ws.at[3 + i], wr.at[3 + i], xs[i]) for i in range(3)]
    wl = [pltpu.make_async_copy(PD.at[:, :, xcols[0]], OD, loc.at[8])]

    sends = []
    gots = {}

    def zsend(d, k, h):
        slot = (slot_r if d == 0 else slot_l)(k)
        rows = rows_of(slot, h)
        r = remote(A.at[slot, h, rows], V.at[d, k - 1, h, rows], zs.at[d, k - 1, h], zr.at[d, k - 1, h], left if d == 0 else right)
        r.start()
        sends.append(r)
        gots[d, k - 1, h] = r

    def msend(d, k):
        slot = (slot_r if d == 0 else slot_l)(k)
        r = remote(GA.at[slot], GV.at[d, k - 1], ms.at[d, k - 1], mr.at[d, k - 1], left if d == 0 else right)
        r.start()
        sends.append(r)
        gots[d, k - 1, 2] = r

    def add(slot, h, more, dst):
        @pl.loop(0, TOK, step=32)
        def _(at):
            rows = pl.ds(pl.multiple_of(at, 32), 32)
            total = A[slot, h, rows].astype(F32)
            for d, k in more:
                total += V[d, k, h, rows].astype(F32)
            dst[rows] = total.astype(BF)

    def add_gate(slot, more):
        total = GA[slot].astype(F32)
        for d, k in more:
            total += GV[d, k].astype(F32)
        return total.astype(BF)

    def unpack(p, first=False):
        slots = pair_slots(p)
        hot, weight, eqs = selection(M[slots[0]], M[slots[1]], z * 8, c)
        rows = pl.ds(p * 16, 16)
        over = (((0,), (0,)), ((), ()))
        gate = jnp.sum(weight, axis=1, keepdims=True)
        ways = (routes(slots, 0, weight, c, gate), routes(slots, 1, hot, c))
        if first:
            for r in core:
                r.wait_recv()
        for n, w in enumerate(ways):
            v = jnp.concatenate([b[n, q, rows] for b in (OB, OR) for q in range(NY)], axis=0)
            u = lax.dot_general(w, v, over, preferred_element_type=F32).astype(BF)
            for h, slot in enumerate(slots):
                A[slot, n] = u[h * TOK : (h + 1) * TOK]
        dots = jnp.concatenate([b[q, rows] for b in (SB, SR) for q in range(NY)], axis=0)
        for h, slot in enumerate(slots):
            gp = [jnp.sum(jnp.where(eq, dots, 0.0), axis=0, keepdims=True) for eq in eqs[h]]
            GA[slot] = jnp.concatenate(gp + [jnp.zeros((12, TOK), F32)], axis=0).astype(BF)

    near.wait()
    unpack(0, True)
    for k in range(8, 0, -1):
        order = [(0, 1), (1, 0), (0, 0), (1, 1)] if k == 7 else [(0, 0), (1, 1)] if k == 8 else [(0, 0), (1, 0), (0, 1), (1, 1)]
        for d, h in order:
            slot = (slot_r if d == 0 else slot_l)(k)
            if (d, k, h) in gots:
                gots[d, k, h].wait_recv()
                came = PACKED.get(((slot_r if d == 0 else slot_l)(k + 1), h))
                if came is None:
                    add(slot, h, [(d, k)], A.at[slot, h])
                elif came == 8:
                    total = A[slot, h, 32:80].astype(F32) + V[d, k, h, 0:48].astype(F32)
                    A[slot, h, 32:80] = total.astype(BF)
                else:
                    hot = ahead(M[slot], z, d)
                    total = lax.dot_general(hot, V[d, k, h, 0:80], (((0,), (0,)), ((), ())), preferred_element_type=F32)
                    A[slot, h] = (total + A[slot, h].astype(F32)).astype(BF)
            zsend(d, k, h)
        for d in (0, 1) if k < 8 else (0,):
            slot = (slot_r if d == 0 else slot_l)(k)
            if (d, k, 2) in gots:
                gots[d, k, 2].wait_recv()
                GA[slot] = add_gate(slot, [(d, k)])
            msend(d, k)
        if k > 1:
            unpack(k - 1)
        if k in (7, 6):
            weigh(2 * (7 - k))
            weigh(2 * (7 - k) + 1)
        if k == 6:
            for r in w1 + wl:
                r.start()
        if k == 2:
            for r in wl:
                r.wait()
            for r in w1:
                r.wait_recv()

            @pl.loop(0, D, step=32)
            def _(at):
                rows = pl.ds(pl.multiple_of(at, 32), 32)
                total = PU[y, rows].astype(F32)
                for i in range(3):
                    total += RU[i, rows].astype(F32)
                SU[rows] = total.astype(BF)

            @pl.loop(0, NY)
            def _(j):
                @pl.loop(0, FF, step=64)
                def _(at):
                    rows = pl.ds(pl.multiple_of(at, 64), 64)
                    total = OD[j, rows].astype(F32)
                    for i in range(3):
                        total += RD[i, j, rows].astype(F32)
                    SD[j, rows] = total.astype(BF)

            w2 = [remote(SU.at[xcols[i + 1]], RU2.at[i], ws.at[6 + i], wr.at[6 + i], xs[i]) for i in range(3)]
            w2 += [remote(SD.at[yat[i + 1]], RD2.at[i], ws.at[9 + i], wr.at[9 + i], ys[i]) for i in range(3)]
            for r in w2:
                r.start()
        if k == 1:
            for r in w2:
                r.wait_recv()

            @pl.loop(0, 256, step=32)
            def _(at):
                rows = pl.ds(pl.multiple_of(at, 32), 32)
                total = SU[pl.ds(pl.multiple_of(x * 256 + at, 32), 32)].astype(F32)
                for i in range(3):
                    total += RU2[i, rows].astype(F32)
                SU2[rows] = total.astype(BF)

            @pl.loop(0, FF, step=64)
            def _(at):
                rows = pl.ds(pl.multiple_of(at, 64), 64)
                total = SD[y, rows].astype(F32)
                for i in range(3):
                    total += RD2[i, rows].astype(F32)
                SD2[rows] = total.astype(BF)

            theirs = pl.ds(pl.multiple_of((1 - c) * 128, 128), 128)
            w3 = [
                remote(SU2.at[theirs], RU3, ws.at[12], wr.at[12], sib),
                remote(SD2.at[:, theirs], RD3, ws.at[13], wr.at[13], sib),
            ]
            for r in w3:
                r.start()
    for r in w3:
        r.wait_recv()
    mine = pl.ds(pl.multiple_of(c * 128, 128), 128)
    last = [
        pltpu.make_async_copy(SU2.at[mine], UG.at[c], loc.at[9]),
        pltpu.make_async_copy(RU3, UG.at[1 - c], loc.at[10]),
        pltpu.make_async_copy(SD2.at[:, mine], DG.at[c], loc.at[11]),
        pltpu.make_async_copy(RD3, DG.at[1 - c], loc.at[12]),
    ]
    for r in last:
        r.start()
    for h in (0, 1):
        for d in (0, 1):
            gots[d, 0, h].wait_recv()
        add(0, h, [(0, 0), (1, 0)], FV.at[h])
        r = pltpu.make_async_copy(FV.at[h], F.at[h], loc.at[13 + h])
        r.start()
        last.append(r)
    for d in (0, 1):
        gots[d, 0, 2].wait_recv()
    GF[...] = add_gate(0, [(0, 0), (1, 0)])
    r = pltpu.make_async_copy(GF, GO, loc.at[15])
    r.start()
    last.append(r)
    for r in sends + w1 + w2 + w3 + core:
        r.wait_send()
    for r in last:
        r.wait()


def out_kernel(F, G, UG, DG, mixed, back, gate, upg, dng):
    mixed[...] = F[0]
    back[...] = F[1]
    gate[...] = G[0:TOP]
    upg[...] = UG[...].astype(F32)
    dng[...] = DG[...].astype(F32)


def shards(tokens, expert_ids, gates, w_up, w_down, out_grad):
    dma = pltpu.SemaphoreType.DMA
    sd = jax.ShapeDtypeStruct
    vm = pltpu.VMEM
    X, M, WU, WD = pl.pallas_call(
        ag_kernel,
        name="gather",
        out_shape=(
            sd((3, NY, 256, D), BF),
            sd((NZ, 16, TOK), BF),
            sd((NY, D, FF), BF),
            sd((NY, FF, D), BF),
        ),
        in_specs=[ANY, ANY, VM, VM, ANY, ANY],
        out_specs=[ANY] * 4,
        scratch_shapes=[vm((NZ, 2, TOK, D), BF), vm((NZ, 16, TOK), BF), vm((8, 2, 3, NY, 16, D), BF), vm((4, 80, D), BF)]
        + [dma((2, 8, 2))] * 2 + [dma((2, 8))] * 2 + [dma((8,))] * 3 + [dma((14,))] * 2 + [dma((5,))],
        compiler_params=pltpu.CompilerParams(collective_id=1, has_side_effects=True, vmem_limit_bytes=60 << 20),
    )(tokens, out_grad, expert_ids.T, gates.T, w_up, w_down)

    parts = pl.pallas_call(
        rs_kernel,
        name="scatter",
        out_shape=(
            sd((2, TOK, D), BF),
            sd((16, TOK), BF),
            sd((2, D // 8, FF), BF),
            sd((2, FF, D // 8), BF),
        ),
        in_specs=[ANY] * 4,
        out_specs=[ANY] * 4,
        scratch_shapes=[
            vm((3, NY, 256, D), BF), vm((2, D, FF), BF), vm((2, FF, D), BF),
            vm((2, NY, 256, D), BF), vm((2, NY, 128, D), BF), vm((NY, 256, 128), F32), vm((NY, 128, 128), F32),
            vm((NY, 256, FF), BF), vm((NY, 256, FF), BF), vm((NY, D, FF), BF), vm((NY, FF, D), BF),
            vm((NZ, 16, TOK), BF), vm((NZ, 2, TOK, D), BF), vm((2, 8, 2, TOK, D), BF),
            vm((NZ, 16, TOK), BF), vm((2, 8, 16, TOK), BF), vm((2, TOK, D), BF), vm((16, TOK), BF),
            vm((3, D, FF), BF), vm((D, FF), BF), vm((3, 256, FF), BF), vm((256, FF), BF), vm((128, FF), BF),
            vm((3, NY, FF, 256), BF), vm((NY, FF, 256), BF), vm((NY, FF, 256), BF), vm((3, FF, 256), BF), vm((FF, 256), BF), vm((FF, 128), BF),
        ] + [dma((2, 8, 2))] * 2 + [dma((2, 8))] * 2 + [dma((8,))] * 2 + [dma((14,))] * 2 + [dma((16,)), dma((NY, 3))],
        compiler_params=pltpu.CompilerParams(collective_id=2, has_side_effects=True, vmem_limit_bytes=60 << 20),
    )(X, M, WU, WD)

    mixed, back, gate, upg, dng = pl.pallas_call(
        out_kernel,
        name="outputs",
        out_shape=(
            sd((TOK, D), BF),
            sd((TOK, D), BF),
            sd((TOP, TOK), BF),
            sd((2, D // 8, FF), F32),
            sd((2, FF, D // 8), F32),
        ),
        in_specs=[VM] * 4,
        out_specs=[VM] * 5,
    )(*parts)
    return mixed, back, gate.T, upg, dng


def solution(mesh):
    rows = P(("dp", "expert"), None)
    up, down = P("expert", "dp", None), P("expert", None, "dp")
    return jax.shard_map(
        shards,
        mesh=mesh,
        in_specs=(rows, rows, rows, up, down, rows),
        out_specs=(rows, rows, rows, up, down),
        check_vma=False,
    )
```

```python
import jax
import jax.numpy as jnp
from jax import lax
from jax.experimental import pallas as pl
from jax.experimental.pallas import tpu as pltpu
from jax.sharding import PartitionSpec as P

NX, NY, NZ = 4, 4, 16
TOK, D, FF, TOP = 128, 1024, 512, 4
BF = jnp.bfloat16
F32 = jnp.float32
MESH_ID = pl.DeviceIdType.MESH
ANY = pl.BlockSpec(memory_space=pl.ANY)
VM = pl.BlockSpec(memory_space=pltpu.VMEM)


def slot_r(k):
    return 15 if k == 8 else 2 * k - 1


def slot_l(k):
    return 15 if k == 8 else 2 * k


def places():
    dp, ex = lax.axis_index("dp"), lax.axis_index("expert")
    x, c = lax.div(dp, 2), lax.rem(dp, 2)
    z, y = lax.div(ex, NY), lax.rem(ex, NY)
    right = (dp, lax.rem(z + 1, NZ) * NY + y)
    left = (dp, lax.rem(z + NZ - 1, NZ) * NY + y)
    sib = (x * 2 + 1 - c, ex)
    xs = [(lax.rem(x + i, NX) * 2 + c, ex) for i in range(1, NX)]
    ys = [(dp, z * NY + lax.rem(y + i, NY)) for i in range(1, NY)]
    return x, y, z, c, right, left, sib, xs, ys


def greet(partners):
    barrier = pltpu.get_barrier_semaphore()
    for p in partners:
        pl.semaphore_signal(barrier, inc=1, device_id=p, device_id_type=MESH_ID)
    pl.semaphore_wait(barrier, len(partners))


def remote(src, dst, send, recv, to):
    return pltpu.make_async_remote_copy(
        src_ref=src, dst_ref=dst, send_sem=send, recv_sem=recv, device_id=to, device_id_type=MESH_ID
    )


def selection(meta_a, meta_b, first, core):
    hot, weight, eqs = [], [], []
    for h, m in enumerate((meta_a, meta_b)):
        m = m.astype(F32)
        at = m[0:4].astype(jnp.int32) - first
        rank = m[4:8].astype(jnp.int32)
        row = jnp.where((at & 1) == core, 0, 64) + (at >> 1) * 16 + h * 8 + rank
        row = jnp.where((at >= 0) & (at < 8), row, -1)
        r = lax.broadcasted_iota(jnp.int32, (128, TOK), 0)
        eq = [r == row[k : k + 1] for k in range(TOP)]
        hot.append(sum(jnp.where(e, 1.0, 0.0) for e in eq))
        weight.append(sum(jnp.where(e, m[8 + k : 9 + k], 0.0) for k, e in enumerate(eq)))
        eqs.append(eq)
    return jnp.concatenate(hot, axis=1), jnp.concatenate(weight, axis=1), eqs


def pair_slots(p):
    return (0, 15) if p == 0 else (2 * p - 1, 2 * p)


PACKED = {(11, 1): 0, (12, 0): 0, (13, 0): 0, (13, 1): 8, (14, 0): 8, (14, 1): 0, (15, 0): 8, (15, 1): 8}
ROWS = {None: TOK, 0: 80, 8: 48}


def rows_of(slot, h):
    return pl.ds(0, ROWS[PACKED.get((slot, h))])


def blocks_of(slot, h):
    return [rows_of(slot, h)] if (slot, h) in PACKED else [pl.ds(0, 64), pl.ds(64, 64)]


def ahead(m, z, d):
    m = m.astype(F32)
    ids, rank = m[0:4].astype(jnp.int32), m[4:8].astype(jnp.int32)
    one, two = (lax.rem(z + (n if d == 0 else NZ - n), NZ) for n in (1, 2))
    plane = ids >> 3
    row = jnp.where(plane == one, 0, jnp.where(plane == two, 40, -1000)) + (ids & 7) * 5 + rank
    r = lax.broadcasted_iota(jnp.int32, (80, TOK), 0)
    return sum(jnp.where(r == row[k : k + 1], 1.0, 0.0) for k in range(TOP)).astype(BF)


def settle(h, first, c):
    r = lax.broadcasted_iota(jnp.int32, (128, TOK), 0)
    rank = r & 7
    at = (((r >> 4) & 3) * 2 + ((r >> 6) ^ c)) * 5 + rank + first
    at = jnp.where((((r >> 3) & 1) == h) & (rank < 5), at, -1)
    return jnp.where(lax.broadcasted_iota(jnp.int32, (128, TOK), 1) == at, 1.0, 0.0)


def routes(slots, n, dense, c, gate=None):
    made = []
    for h, slot in enumerate(slots):
        kind = PACKED.get((slot, n))
        if kind is None:
            made.append(dense[:, h * TOK : (h + 1) * TOK])
        else:
            made.append(settle(h, kind, c) if gate is None else settle(h, kind, c) * gate)
    return jnp.concatenate(made, axis=1).astype(BF)


def ag_kernel(
    tok, cot, ids, gates, wu, wd, X, MO, WU, WD,
    T, M, B, Q, zs, zr, ms, mr, ps, pr, lp, ws, wr, loc,
):
    x, y, z, c, right, left, sib, xs, ys = places()
    greet([right, left, sib] + xs + ys)
    own = (tok, cot)
    steps = {}

    def zsend(d, k, h, part):
        slot = slot_r if d == 0 else slot_l
        kind, rows = PACKED.get((slot(k), h)), blocks_of(slot(k), h)[part]
        if kind == 0:
            past, n = slot(k - 1), 2 * d + k - 6
            Q[n] = jnp.dot(ahead(M[past], z, d), T[past, h], preferred_element_type=F32).astype(BF)
            src = Q.at[n]
        elif kind == 8:
            src = T.at[slot(k - 1), h, pl.ds(32, 48)]
        else:
            src = own[h].at[rows] if k == 1 else T.at[slot(k - 1), h, rows]
        at = (d, k - 1, h, part)
        r = remote(src, T.at[slot(k), h, rows], zs.at[at], zr.at[at], right if d == 0 else left)
        r.start()
        steps[d, k, h, part] = r

    def msend(d, k):
        slot = slot_r if d == 0 else slot_l
        src = M.at[0 if k == 1 else slot(k - 1)]
        r = remote(src, M.at[slot(k)], ms.at[d, k - 1], mr.at[d, k - 1], right if d == 0 else left)
        r.start()
        steps[d, k, 2] = r

    for h in (0, 1):
        for part in (0, 1):
            for d in (0, 1):
                zsend(d, 1, h, part)
    rows1 = pl.ds(pl.multiple_of(x * 256 + c * 128, 128), 128)
    rows2 = pl.ds(pl.multiple_of(x * 256, 256), 256)
    wl = [
        pltpu.make_async_copy(wu.at[c], WU.at[y, rows1], loc.at[0]),
        pltpu.make_async_copy(wd.at[c], WD.at[y, :, rows1], loc.at[1]),
    ]
    wc = [
        remote(wu.at[1 - c], WU.at[y, rows1], ws.at[0], wr.at[0], sib),
        remote(wd.at[1 - c], WD.at[y, :, rows1], ws.at[1], wr.at[1], sib),
    ]
    own_local = [
        pltpu.make_async_copy(tok, T.at[0, 0], loc.at[2]),
        pltpu.make_async_copy(cot, T.at[0, 1], loc.at[3]),
    ]
    for r in wl + wc + own_local:
        r.start()
    e = lax.broadcasted_iota(jnp.int32, (128, TOK), 0)
    eq = [e == ids[k : k + 1] for k in range(TOP)]
    hot = sum(jnp.where(q, 1.0, 0.0) for q in eq)
    earlier = jnp.where(e < lax.broadcasted_iota(jnp.int32, (128, TOK), 1), 1.0, 0.0)
    before = jnp.dot(hot.astype(BF), earlier.astype(BF), preferred_element_type=F32)
    ranks = [jnp.sum(jnp.where(q, before, 0.0), axis=0, keepdims=True) for q in eq]
    M[0] = jnp.concatenate(
        [ids[...].astype(F32)] + ranks + [gates[...].astype(F32), jnp.zeros((4, TOK), F32)], axis=0
    ).astype(BF)
    for d in (0, 1):
        msend(d, 1)
    for (slot, h), kind in PACKED.items():
        T[slot, h, ROWS[kind] :] = jnp.zeros((TOK - ROWS[kind], D), BF)
    for r in wl:
        r.wait()
    for r in wc:
        r.wait_recv()
    w1 = [remote(WU.at[y, rows2], WU.at[y, rows2], ws.at[2 + i], wr.at[2 + i], xs[i]) for i in range(3)]
    w1 += [remote(WD.at[y, :, rows2], WD.at[y, :, rows2], ws.at[5 + i], wr.at[5 + i], ys[i]) for i in range(3)]
    for r in w1:
        r.start()
    w2 = [remote(WU.at[y], WU.at[y], ws.at[8 + i], wr.at[8 + i], ys[i]) for i in range(3)]
    w2 += [remote(WD.at[:, :, rows2], WD.at[:, :, rows2], ws.at[11 + i], wr.at[11 + i], xs[i]) for i in range(3)]

    packed = []

    def choose(p):
        a, b = pair_slots(p)
        hot, weight, _ = selection(M[a], M[b], z * 8, c)
        return routes((a, b), 0, hot, c), routes((a, b), 1, hot, c), jnp.sum(weight, axis=1, keepdims=True)

    def pack(p, chosen):
        a, b = pair_slots(p)
        for_tok, for_cot, gate = chosen
        t = jnp.dot(for_tok, jnp.concatenate([T[a, 0], T[b, 0]], axis=0), preferred_element_type=F32)
        g = jnp.dot(for_cot, jnp.concatenate([T[a, 1], T[b, 1]], axis=0), preferred_element_type=F32)
        for n, v in enumerate((t.astype(BF), g.astype(BF), (g * gate).astype(BF))):
            for q in range(8):
                B[p, q // 4, n, q % 4] = v[q * 16 : q * 16 + 16]
        here = pltpu.make_async_copy(B.at[p, 0], X.at[:, :, pl.ds(p * 16, 16)], lp.at[p])
        there = remote(B.at[p, 1], X.at[:, :, pl.ds(128 + p * 16, 16)], ps.at[p], pr.at[p], sib)
        here.start()
        there.start()
        packed.append((here, there))

    for k in range(1, 9):
        for d in (0, 1):
            if (d, k, 2) not in steps:
                continue
            steps[d, k, 2].wait_recv()
            if k < 7 or (k == 7 and d == 0):
                msend(d, k + 1)
        chosen = choose(0) if k == 8 else None
        for h in (0, 1):
            for part in (0, 1):
                for d in (0, 1):
                    if (d, k, h, part) not in steps:
                        continue
                    steps[d, k, h, part].wait_recv()
                    slot = slot_r if d == 0 else slot_l
                    if k == 8 or (k == 7 and h != d):
                        continue
                    if (slot(k + 1), h) not in PACKED:
                        zsend(d, k + 1, h, part)
                    elif part == len(blocks_of(slot(k), h)) - 1:
                        zsend(d, k + 1, h, 0)
        if k == 1:
            for r in own_local:
                r.wait()
        pack(k % 8, chosen or choose(k))
        if k == 1:
            for r in w1:
                r.wait_recv()
            for r in w2:
                r.start()
    out = pltpu.make_async_copy(M, MO, loc.at[4])
    out.start()
    for r in w2:
        r.wait_recv()
    for here, there in packed:
        here.wait()
        there.wait_recv()
    for r in list(steps.values()) + wc + w1 + w2 + [there for _, there in packed]:
        r.wait_send()
    out.wait()


def rs_kernel(
    X, MI, WU, WD, F, GO, UG, DG,
    XV, WUV, WDV, OB, OR, SB, SR, AC, PG, PU, PD,
    M, A, V, GA, GV, FV, GF, RU, SU, RU2, SU2, RU3, RD, OD, SD, RD2, SD2, RD3,
    zs, zr, ms, mr, cs, cr, ws, wr, loc, ld,
):
    x, y, z, c, right, left, sib, xs, ys = places()
    loads = {}

    def load(e):
        loads[e] = [
            pltpu.make_async_copy(X.at[:, e], XV.at[:, e], ld.at[e, 0]),
            pltpu.make_async_copy(WU.at[e], WUV.at[e % 2], ld.at[e, 1]),
            pltpu.make_async_copy(WD.at[e], WDV.at[e % 2], ld.at[e, 2]),
        ]
        for r in loads[e]:
            r.start()

    load(0)
    load(1)
    near = pltpu.make_async_copy(MI, M, loc.at[0])
    near.start()
    greet([right, left, sib] + xs + ys)
    core = []
    for e in range(NY):
        for r in loads[e]:
            r.wait()
        rows, cot, scaled, wu, wd = XV[0, e], XV[1, e], XV[2, e], WUV[e % 2], WDV[e % 2]
        pre = jnp.dot(rows, wu, preferred_element_type=F32)
        t = jnp.tanh(0.7978845608 * (pre + 0.044715 * pre * pre * pre))
        act = (0.5 * pre * (1.0 + t)).astype(BF)
        slope = 0.5 * (1.0 + t) + 0.5 * pre * (1.0 - t * t) * (0.7978845608 * (1.0 + 0.134145 * pre * pre))
        act_grad = lax.dot_general(scaled, wd, (((1,), (1,)), ((), ())), preferred_element_type=F32)
        pre_grad = (act_grad * slope).astype(BF)
        outs = jnp.dot(act, wd, preferred_element_type=F32).astype(BF)
        OB[0, e] = outs
        SB[e] = jnp.broadcast_to(jnp.sum(cot.astype(F32) * outs.astype(F32), axis=1, keepdims=True), (256, 128))
        OB[1, e] = lax.dot_general(pre_grad, wu, (((1,), (1,)), ((), ())), preferred_element_type=F32).astype(BF)
        AC[e] = act
        PG[e] = pre_grad
        pair = [
            remote(OB.at[:, e, pl.ds(128, 128)], OR.at[:, e], cs.at[e], cr.at[e], sib),
            remote(SB.at[e, pl.ds(128, 128)], SR.at[e], cs.at[4 + e], cr.at[4 + e], sib),
        ]
        for r in pair:
            r.start()
        core += pair
        if e < 2:
            load(e + 2)

    def weigh(e):
        over = (((0,), (0,)), ((), ()))
        PU[e] = lax.dot_general(XV[0, e], PG[e], over, preferred_element_type=F32).astype(BF)
        PD[e] = lax.dot_general(AC[e], XV[2, e], over, preferred_element_type=F32).astype(BF)

    xcols = [pl.ds(pl.multiple_of(lax.rem(x + i, NX) * 256, 256), 256) for i in range(NX)]
    yat = [lax.rem(y + i, NY) for i in range(NY)]
    w1 = [remote(PU.at[yat[i + 1]], RU.at[i], ws.at[i], wr.at[i], ys[i]) for i in range(3)]
    w1 += [remote(PD.at[:, :, xcols[i + 1]], RD.at[i], ws.at[3 + i], wr.at[3 + i], xs[i]) for i in range(3)]
    wl = [pltpu.make_async_copy(PD.at[:, :, xcols[0]], OD, loc.at[8])]

    sends = []
    gots = {}

    def zsend(d, k, h, part):
        slot = (slot_r if d == 0 else slot_l)(k)
        rows = blocks_of(slot, h)[part]
        at = (d, k - 1, h, part)
        r = remote(A.at[slot, h, rows], V.at[d, k - 1, h, rows], zs.at[at], zr.at[at], left if d == 0 else right)
        r.start()
        sends.append(r)
        gots[d, k - 1, h, part] = r

    def msend(d, k):
        slot = (slot_r if d == 0 else slot_l)(k)
        r = remote(GA.at[slot], GV.at[d, k - 1], ms.at[d, k - 1], mr.at[d, k - 1], left if d == 0 else right)
        r.start()
        sends.append(r)
        gots[d, k - 1, 2, 0] = r

    def add(slot, h, part, more, dst):
        @pl.loop(part * 64, part * 64 + 64, step=32)
        def _(at):
            rows = pl.ds(pl.multiple_of(at, 32), 32)
            total = A[slot, h, rows].astype(F32)
            for d, k in more:
                total += V[d, k, h, rows].astype(F32)
            dst[rows] = total.astype(BF)

    def add_gate(slot, more):
        total = GA[slot].astype(F32)
        for d, k in more:
            total += GV[d, k].astype(F32)
        return total.astype(BF)

    def unpack(p, first=False):
        slots = pair_slots(p)
        hot, weight, eqs = selection(M[slots[0]], M[slots[1]], z * 8, c)
        rows = pl.ds(p * 16, 16)
        over = (((0,), (0,)), ((), ()))
        gate = jnp.sum(weight, axis=1, keepdims=True)
        ways = (routes(slots, 0, weight, c, gate), routes(slots, 1, hot, c))
        if first:
            for r in core:
                r.wait_recv()
        for n, w in enumerate(ways):
            v = jnp.concatenate([b[n, q, rows] for b in (OB, OR) for q in range(NY)], axis=0)
            u = lax.dot_general(w, v, over, preferred_element_type=F32).astype(BF)
            for h, slot in enumerate(slots):
                A[slot, n] = u[h * TOK : (h + 1) * TOK]
        dots = jnp.concatenate([b[q, rows] for b in (SB, SR) for q in range(NY)], axis=0)
        for h, slot in enumerate(slots):
            gp = [jnp.sum(jnp.where(eq, dots, 0.0), axis=0, keepdims=True) for eq in eqs[h]]
            GA[slot] = jnp.concatenate(gp + [jnp.zeros((12, TOK), F32)], axis=0).astype(BF)

    near.wait()
    unpack(0, True)
    for k in range(8, 0, -1):
        order = [(0, 1), (1, 0), (0, 0), (1, 1)] if k == 7 else [(0, 0), (1, 1)] if k == 8 else [(0, 0), (1, 0), (0, 1), (1, 1)]
        for d, h, part in [(d, h, part) for h in (0, 1) for part in (0, 1) for d in (0, 1)] if k < 7 else [(d, h, 0) for d, h in order]:
            slot = (slot_r if d == 0 else slot_l)(k)
            far = ((slot_r if d == 0 else slot_l)(k + 1), h) if k < 8 else None
            if part == len(blocks_of(slot, h)):
                continue
            if k < 7 and far not in PACKED:
                gots[d, k, h, part].wait_recv()
                add(slot, h, part, [(d, k)], A.at[slot, h])
            elif part == 0 and (d, k, h, 0) in gots:
                gots[d, k, h, 0].wait_recv()
                if PACKED[far] == 8:
                    total = A[slot, h, 32:80].astype(F32) + V[d, k, h, 0:48].astype(F32)
                    A[slot, h, 32:80] = total.astype(BF)
                else:
                    hot = ahead(M[slot], z, d)
                    total = lax.dot_general(hot, V[d, k, h, 0:80], (((0,), (0,)), ((), ())), preferred_element_type=F32)
                    A[slot, h] = (total + A[slot, h].astype(F32)).astype(BF)
            zsend(d, k, h, part)
        for d in (0, 1) if k < 8 else (0,):
            slot = (slot_r if d == 0 else slot_l)(k)
            if (d, k, 2, 0) in gots:
                gots[d, k, 2, 0].wait_recv()
                GA[slot] = add_gate(slot, [(d, k)])
            msend(d, k)
        if k > 1:
            unpack(k - 1)
        if k in (7, 6):
            weigh(2 * (7 - k))
            weigh(2 * (7 - k) + 1)
        if k == 6:
            for r in w1 + wl:
                r.start()
        if k == 2:
            for r in wl:
                r.wait()
            for r in w1:
                r.wait_recv()

            @pl.loop(0, D, step=32)
            def _(at):
                rows = pl.ds(pl.multiple_of(at, 32), 32)
                total = PU[y, rows].astype(F32)
                for i in range(3):
                    total += RU[i, rows].astype(F32)
                SU[rows] = total.astype(BF)

            @pl.loop(0, NY)
            def _(j):
                @pl.loop(0, FF, step=64)
                def _(at):
                    rows = pl.ds(pl.multiple_of(at, 64), 64)
                    total = OD[j, rows].astype(F32)
                    for i in range(3):
                        total += RD[i, j, rows].astype(F32)
                    SD[j, rows] = total.astype(BF)

            w2 = [remote(SU.at[xcols[i + 1]], RU2.at[i], ws.at[6 + i], wr.at[6 + i], xs[i]) for i in range(3)]
            w2 += [remote(SD.at[yat[i + 1]], RD2.at[i], ws.at[9 + i], wr.at[9 + i], ys[i]) for i in range(3)]
            for r in w2:
                r.start()
        if k == 1:
            for r in w2:
                r.wait_recv()

            @pl.loop(0, 256, step=32)
            def _(at):
                rows = pl.ds(pl.multiple_of(at, 32), 32)
                total = SU[pl.ds(pl.multiple_of(x * 256 + at, 32), 32)].astype(F32)
                for i in range(3):
                    total += RU2[i, rows].astype(F32)
                SU2[rows] = total.astype(BF)

            @pl.loop(0, FF, step=64)
            def _(at):
                rows = pl.ds(pl.multiple_of(at, 64), 64)
                total = SD[y, rows].astype(F32)
                for i in range(3):
                    total += RD2[i, rows].astype(F32)
                SD2[rows] = total.astype(BF)

            theirs = pl.ds(pl.multiple_of((1 - c) * 128, 128), 128)
            w3 = [
                remote(SU2.at[theirs], RU3, ws.at[12], wr.at[12], sib),
                remote(SD2.at[:, theirs], RD3, ws.at[13], wr.at[13], sib),
            ]
            for r in w3:
                r.start()
    for r in w3:
        r.wait_recv()
    mine = pl.ds(pl.multiple_of(c * 128, 128), 128)
    last = [
        pltpu.make_async_copy(SU2.at[mine], UG.at[c], loc.at[9]),
        pltpu.make_async_copy(RU3, UG.at[1 - c], loc.at[10]),
        pltpu.make_async_copy(SD2.at[:, mine], DG.at[c], loc.at[11]),
        pltpu.make_async_copy(RD3, DG.at[1 - c], loc.at[12]),
    ]
    for r in last:
        r.start()
    for h in (0, 1):
        for part in (0, 1):
            for d in (0, 1):
                gots[d, 0, h, part].wait_recv()
            add(0, h, part, [(0, 0), (1, 0)], FV.at[h])
        r = pltpu.make_async_copy(FV.at[h], F.at[h], loc.at[13 + h])
        r.start()
        last.append(r)
    for d in (0, 1):
        gots[d, 0, 2, 0].wait_recv()
    GF[...] = add_gate(0, [(0, 0), (1, 0)])
    r = pltpu.make_async_copy(GF, GO, loc.at[15])
    r.start()
    last.append(r)
    for r in sends + w1 + w2 + w3 + core:
        r.wait_send()
    for r in last:
        r.wait()


def out_kernel(F, G, UG, DG, mixed, back, gate, upg, dng):
    mixed[...] = F[0]
    back[...] = F[1]
    gate[...] = G[0:TOP]
    upg[...] = UG[...].astype(F32)
    dng[...] = DG[...].astype(F32)


def shards(tokens, expert_ids, gates, w_up, w_down, out_grad):
    dma = pltpu.SemaphoreType.DMA
    sd = jax.ShapeDtypeStruct
    vm = pltpu.VMEM
    X, M, WU, WD = pl.pallas_call(
        ag_kernel,
        name="gather",
        out_shape=(
            sd((3, NY, 256, D), BF),
            sd((NZ, 16, TOK), BF),
            sd((NY, D, FF), BF),
            sd((NY, FF, D), BF),
        ),
        in_specs=[ANY, ANY, VM, VM, ANY, ANY],
        out_specs=[ANY] * 4,
        scratch_shapes=[vm((NZ, 2, TOK, D), BF), vm((NZ, 16, TOK), BF), vm((8, 2, 3, NY, 16, D), BF), vm((4, 80, D), BF)]
        + [dma((2, 8, 2, 2))] * 2 + [dma((2, 8))] * 2 + [dma((8,))] * 3 + [dma((14,))] * 2 + [dma((5,))],
        compiler_params=pltpu.CompilerParams(collective_id=1, has_side_effects=True, vmem_limit_bytes=60 << 20),
    )(tokens, out_grad, expert_ids.T, gates.T, w_up, w_down)

    parts = pl.pallas_call(
        rs_kernel,
        name="scatter",
        out_shape=(
            sd((2, TOK, D), BF),
            sd((16, TOK), BF),
            sd((2, D // 8, FF), BF),
            sd((2, FF, D // 8), BF),
        ),
        in_specs=[ANY] * 4,
        out_specs=[ANY] * 4,
        scratch_shapes=[
            vm((3, NY, 256, D), BF), vm((2, D, FF), BF), vm((2, FF, D), BF),
            vm((2, NY, 256, D), BF), vm((2, NY, 128, D), BF), vm((NY, 256, 128), F32), vm((NY, 128, 128), F32),
            vm((NY, 256, FF), BF), vm((NY, 256, FF), BF), vm((NY, D, FF), BF), vm((NY, FF, D), BF),
            vm((NZ, 16, TOK), BF), vm((NZ, 2, TOK, D), BF), vm((2, 8, 2, TOK, D), BF),
            vm((NZ, 16, TOK), BF), vm((2, 8, 16, TOK), BF), vm((2, TOK, D), BF), vm((16, TOK), BF),
            vm((3, D, FF), BF), vm((D, FF), BF), vm((3, 256, FF), BF), vm((256, FF), BF), vm((128, FF), BF),
            vm((3, NY, FF, 256), BF), vm((NY, FF, 256), BF), vm((NY, FF, 256), BF), vm((3, FF, 256), BF), vm((FF, 256), BF), vm((FF, 128), BF),
        ] + [dma((2, 8, 2, 2))] * 2 + [dma((2, 8))] * 2 + [dma((8,))] * 2 + [dma((14,))] * 2 + [dma((16,)), dma((NY, 3))],
        compiler_params=pltpu.CompilerParams(collective_id=2, has_side_effects=True, vmem_limit_bytes=60 << 20),
    )(X, M, WU, WD)

    mixed, back, gate, upg, dng = pl.pallas_call(
        out_kernel,
        name="outputs",
        out_shape=(
            sd((TOK, D), BF),
            sd((TOK, D), BF),
            sd((TOP, TOK), BF),
            sd((2, D // 8, FF), F32),
            sd((2, FF, D // 8), F32),
        ),
        in_specs=[VM] * 4,
        out_specs=[VM] * 5,
    )(*parts)
    return mixed, back, gate.T, upg, dng


def solution(mesh):
    rows = P(("dp", "expert"), None)
    up, down = P("expert", "dp", None), P("expert", None, "dp")
    return jax.shard_map(
        shards,
        mesh=mesh,
        in_specs=(rows, rows, rows, up, down, rows),
        out_specs=(rows, rows, rows, up, down),
        check_vma=False,
    )
```

```python
import jax
import jax.numpy as jnp
from jax import lax
from jax.experimental import pallas as pl
from jax.experimental.pallas import tpu as pltpu
from jax.sharding import PartitionSpec as P

NX, NY, NZ = 4, 4, 16
TOK, D, FF, TOP = 128, 1024, 512, 4
BF = jnp.bfloat16
F32 = jnp.float32
MESH_ID = pl.DeviceIdType.MESH
ANY = pl.BlockSpec(memory_space=pl.ANY)
VM = pl.BlockSpec(memory_space=pltpu.VMEM)


def slot_r(k):
    return 15 if k == 8 else 2 * k - 1


def slot_l(k):
    return 15 if k == 8 else 2 * k


def places():
    dp, ex = lax.axis_index("dp"), lax.axis_index("expert")
    x, c = lax.div(dp, 2), lax.rem(dp, 2)
    z, y = lax.div(ex, NY), lax.rem(ex, NY)
    right = (dp, lax.rem(z + 1, NZ) * NY + y)
    left = (dp, lax.rem(z + NZ - 1, NZ) * NY + y)
    sib = (x * 2 + 1 - c, ex)
    xs = [(lax.rem(x + i, NX) * 2 + c, ex) for i in range(1, NX)]
    ys = [(dp, z * NY + lax.rem(y + i, NY)) for i in range(1, NY)]
    return x, y, z, c, right, left, sib, xs, ys


def greet(partners):
    barrier = pltpu.get_barrier_semaphore()
    for p in partners:
        pl.semaphore_signal(barrier, inc=1, device_id=p, device_id_type=MESH_ID)
    pl.semaphore_wait(barrier, len(partners))


def remote(src, dst, send, recv, to):
    return pltpu.make_async_remote_copy(
        src_ref=src, dst_ref=dst, send_sem=send, recv_sem=recv, device_id=to, device_id_type=MESH_ID
    )


def selection(meta_a, meta_b, first, core):
    hot, weight, eqs = [], [], []
    for h, m in enumerate((meta_a, meta_b)):
        m = m.astype(F32)
        at = m[0:4].astype(jnp.int32) - first
        rank = m[4:8].astype(jnp.int32)
        row = jnp.where((at & 1) == core, 0, 64) + (at >> 1) * 16 + h * 8 + rank
        row = jnp.where((at >= 0) & (at < 8), row, -1)
        r = lax.broadcasted_iota(jnp.int32, (128, TOK), 0)
        eq = [r == row[k : k + 1] for k in range(TOP)]
        hot.append(sum(jnp.where(e, 1.0, 0.0) for e in eq))
        weight.append(sum(jnp.where(e, m[8 + k : 9 + k], 0.0) for k, e in enumerate(eq)))
        eqs.append(eq)
    return jnp.concatenate(hot, axis=1), jnp.concatenate(weight, axis=1), eqs


def pair_slots(p):
    return (0, 15) if p == 0 else (2 * p - 1, 2 * p)


PACKED = {(11, 1): 0, (12, 0): 0, (13, 0): 0, (13, 1): 8, (14, 0): 8, (14, 1): 0, (15, 0): 8, (15, 1): 8}
ROWS = {None: TOK, 0: 80, 8: 48}


def rows_of(slot, h):
    return pl.ds(0, ROWS[PACKED.get((slot, h))])


def ahead(m, z, d):
    m = m.astype(F32)
    ids, rank = m[0:4].astype(jnp.int32), m[4:8].astype(jnp.int32)
    one, two = (lax.rem(z + (n if d == 0 else NZ - n), NZ) for n in (1, 2))
    plane = ids >> 3
    row = jnp.where(plane == one, 0, jnp.where(plane == two, 40, -1000)) + (ids & 7) * 5 + rank
    r = lax.broadcasted_iota(jnp.int32, (80, TOK), 0)
    return sum(jnp.where(r == row[k : k + 1], 1.0, 0.0) for k in range(TOP)).astype(BF)


def settle(h, first, c):
    r = lax.broadcasted_iota(jnp.int32, (128, TOK), 0)
    rank = r & 7
    at = (((r >> 4) & 3) * 2 + ((r >> 6) ^ c)) * 5 + rank + first
    at = jnp.where((((r >> 3) & 1) == h) & (rank < 5), at, -1)
    return jnp.where(lax.broadcasted_iota(jnp.int32, (128, TOK), 1) == at, 1.0, 0.0)


def routes(slots, n, dense, c, gate=None):
    made = []
    for h, slot in enumerate(slots):
        kind = PACKED.get((slot, n))
        if kind is None:
            made.append(dense[:, h * TOK : (h + 1) * TOK])
        else:
            made.append(settle(h, kind, c) if gate is None else settle(h, kind, c) * gate)
    return jnp.concatenate(made, axis=1).astype(BF)


def ag_kernel(
    tok, cot, ids, gates, wu, wd, X, MO, WU, WD,
    T, M, B, Q, zs, zr, ms, mr, ps, pr, lp, ws, wr, loc,
):
    x, y, z, c, right, left, sib, xs, ys = places()
    greet([right, left, sib] + xs + ys)
    own = (tok, cot)
    steps = {}

    def zsend(d, k, h, hot=None):
        slot = slot_r if d == 0 else slot_l
        kind, rows = PACKED.get((slot(k), h)), rows_of(slot(k), h)
        if kind == 0:
            past, n = slot(k - 1), 2 * d + k - 6
            Q[n] = jnp.dot(hot, T[past, h], preferred_element_type=F32).astype(BF)
            src = Q.at[n]
        elif kind == 8:
            src = T.at[slot(k - 1), h, pl.ds(32, 48)]
        else:
            src = own[h] if k == 1 else T.at[slot(k - 1), h]
        r = remote(src, T.at[slot(k), h, rows], zs.at[d, k - 1, h], zr.at[d, k - 1, h], right if d == 0 else left)
        r.start()
        steps[d, k, h] = r

    def msend(d, k):
        slot = slot_r if d == 0 else slot_l
        src = M.at[0 if k == 1 else slot(k - 1)]
        r = remote(src, M.at[slot(k)], ms.at[d, k - 1], mr.at[d, k - 1], right if d == 0 else left)
        r.start()
        steps[d, k, 2] = r

    for h in (0, 1):
        for d in (0, 1):
            zsend(d, 1, h)
    rows1 = pl.ds(pl.multiple_of(x * 256 + c * 128, 128), 128)
    rows2 = pl.ds(pl.multiple_of(x * 256, 256), 256)
    wl = [
        pltpu.make_async_copy(wu.at[c], WU.at[y, rows1], loc.at[0]),
        pltpu.make_async_copy(wd.at[c], WD.at[y, :, rows1], loc.at[1]),
    ]
    wc = [
        remote(wu.at[1 - c], WU.at[y, rows1], ws.at[0], wr.at[0], sib),
        remote(wd.at[1 - c], WD.at[y, :, rows1], ws.at[1], wr.at[1], sib),
    ]
    own_local = [
        pltpu.make_async_copy(tok, T.at[0, 0], loc.at[2]),
        pltpu.make_async_copy(cot, T.at[0, 1], loc.at[3]),
    ]
    for r in wl + wc + own_local:
        r.start()
    e = lax.broadcasted_iota(jnp.int32, (128, TOK), 0)
    eq = [e == ids[k : k + 1] for k in range(TOP)]
    hot = sum(jnp.where(q, 1.0, 0.0) for q in eq)
    earlier = jnp.where(e < lax.broadcasted_iota(jnp.int32, (128, TOK), 1), 1.0, 0.0)
    before = jnp.dot(hot.astype(BF), earlier.astype(BF), preferred_element_type=F32)
    ranks = [jnp.sum(jnp.where(q, before, 0.0), axis=0, keepdims=True) for q in eq]
    M[0] = jnp.concatenate(
        [ids[...].astype(F32)] + ranks + [gates[...].astype(F32), jnp.zeros((4, TOK), F32)], axis=0
    ).astype(BF)
    for d in (0, 1):
        msend(d, 1)
    for (slot, h), kind in PACKED.items():
        T[slot, h, ROWS[kind] :] = jnp.zeros((TOK - ROWS[kind], D), BF)
    for r in wl:
        r.wait()
    for r in wc:
        r.wait_recv()
    w1 = [remote(WU.at[y, rows2], WU.at[y, rows2], ws.at[2 + i], wr.at[2 + i], xs[i]) for i in range(3)]
    w1 += [remote(WD.at[y, :, rows2], WD.at[y, :, rows2], ws.at[5 + i], wr.at[5 + i], ys[i]) for i in range(3)]
    for r in w1:
        r.start()
    w2 = [remote(WU.at[y], WU.at[y], ws.at[8 + i], wr.at[8 + i], ys[i]) for i in range(3)]
    w2 += [remote(WD.at[:, :, rows2], WD.at[:, :, rows2], ws.at[11 + i], wr.at[11 + i], xs[i]) for i in range(3)]

    packed = []

    def choose(p):
        a, b = pair_slots(p)
        hot, weight, _ = selection(M[a], M[b], z * 8, c)
        return routes((a, b), 0, hot, c), routes((a, b), 1, hot, c), jnp.sum(weight, axis=1, keepdims=True)

    def pack(p, chosen):
        a, b = pair_slots(p)
        for_tok, for_cot, gate = chosen
        t = jnp.dot(for_tok, jnp.concatenate([T[a, 0], T[b, 0]], axis=0), preferred_element_type=F32)
        g = jnp.dot(for_cot, jnp.concatenate([T[a, 1], T[b, 1]], axis=0), preferred_element_type=F32)
        for n, v in enumerate((t.astype(BF), g.astype(BF), (g * gate).astype(BF))):
            for q in range(8):
                B[p, q // 4, n, q % 4] = v[q * 16 : q * 16 + 16]
        here = pltpu.make_async_copy(B.at[p, 0], X.at[:, :, pl.ds(p * 16, 16)], lp.at[p])
        there = remote(B.at[p, 1], X.at[:, :, pl.ds(128 + p * 16, 16)], ps.at[p], pr.at[p], sib)
        here.start()
        there.start()
        packed.append((here, there))

    for k in range(1, 9):
        for d in (0, 1):
            if (d, k, 2) not in steps:
                continue
            steps[d, k, 2].wait_recv()
            if k < 7 or (k == 7 and d == 0):
                msend(d, k + 1)
        chosen = choose(0) if k == 8 else None
        hots = [ahead(M[2 * k - 1 + d], z, d) if k in (5, 6) else None for d in (0, 1)]
        for h in (0, 1):
            for d in (0, 1):
                if (d, k, h) not in steps:
                    continue
                steps[d, k, h].wait_recv()
                if k < 7 or (k == 7 and h == d):
                    zsend(d, k + 1, h, hots[d])
        if k == 1:
            for r in own_local:
                r.wait()
        pack(k % 8, chosen or choose(k))
        if k == 1:
            for r in w1:
                r.wait_recv()
            for r in w2:
                r.start()
    out = pltpu.make_async_copy(M, MO, loc.at[4])
    out.start()
    for r in w2:
        r.wait_recv()
    for here, there in packed:
        here.wait()
        there.wait_recv()
    for r in list(steps.values()) + wc + w1 + w2 + [there for _, there in packed]:
        r.wait_send()
    out.wait()


def rs_kernel(
    X, MI, WU, WD, F, GO, UG, DG,
    XV, WUV, WDV, OB, OR, SB, SR, AC, PG, PU, PD,
    M, A, V, GA, GV, FV, GF, RU, SU, RU2, SU2, RU3, RD, OD, SD, RD2, SD2, RD3,
    zs, zr, ms, mr, cs, cr, ws, wr, loc, ld,
):
    x, y, z, c, right, left, sib, xs, ys = places()
    loads = {}

    def load(e):
        loads[e] = [
            pltpu.make_async_copy(X.at[:, e], XV.at[:, e], ld.at[e, 0]),
            pltpu.make_async_copy(WU.at[e], WUV.at[e % 2], ld.at[e, 1]),
            pltpu.make_async_copy(WD.at[e], WDV.at[e % 2], ld.at[e, 2]),
        ]
        for r in loads[e]:
            r.start()

    load(0)
    load(1)
    near = pltpu.make_async_copy(MI, M, loc.at[0])
    near.start()
    greet([right, left, sib] + xs + ys)
    core = []
    for e in range(NY):
        for r in loads[e]:
            r.wait()
        rows, cot, scaled, wu, wd = XV[0, e], XV[1, e], XV[2, e], WUV[e % 2], WDV[e % 2]
        pre = jnp.dot(rows, wu, preferred_element_type=F32)
        t = jnp.tanh(0.7978845608 * (pre + 0.044715 * pre * pre * pre))
        act = (0.5 * pre * (1.0 + t)).astype(BF)
        slope = 0.5 * (1.0 + t) + 0.5 * pre * (1.0 - t * t) * (0.7978845608 * (1.0 + 0.134145 * pre * pre))
        act_grad = lax.dot_general(scaled, wd, (((1,), (1,)), ((), ())), preferred_element_type=F32)
        pre_grad = (act_grad * slope).astype(BF)
        outs = jnp.dot(act, wd, preferred_element_type=F32).astype(BF)
        OB[0, e] = outs
        SB[e] = jnp.broadcast_to(jnp.sum(cot.astype(F32) * outs.astype(F32), axis=1, keepdims=True), (256, 128))
        OB[1, e] = lax.dot_general(pre_grad, wu, (((1,), (1,)), ((), ())), preferred_element_type=F32).astype(BF)
        AC[e] = act
        PG[e] = pre_grad
        pair = [
            remote(OB.at[:, e, pl.ds(128, 128)], OR.at[:, e], cs.at[e], cr.at[e], sib),
            remote(SB.at[e, pl.ds(128, 128)], SR.at[e], cs.at[4 + e], cr.at[4 + e], sib),
        ]
        for r in pair:
            r.start()
        core += pair
        if e < 2:
            load(e + 2)

    def weigh(e):
        over = (((0,), (0,)), ((), ()))
        PU[e] = lax.dot_general(XV[0, e], PG[e], over, preferred_element_type=F32).astype(BF)
        PD[e] = lax.dot_general(AC[e], XV[2, e], over, preferred_element_type=F32).astype(BF)

    xcols = [pl.ds(pl.multiple_of(lax.rem(x + i, NX) * 256, 256), 256) for i in range(NX)]
    yat = [lax.rem(y + i, NY) for i in range(NY)]
    w1 = [remote(PU.at[yat[i + 1]], RU.at[i], ws.at[i], wr.at[i], ys[i]) for i in range(3)]
    w1 += [remote(PD.at[:, :, xcols[i + 1]], RD.at[i], ws.at[3 + i], wr.at[3 + i], xs[i]) for i in range(3)]
    wl = [pltpu.make_async_copy(PD.at[:, :, xcols[0]], OD, loc.at[8])]

    sends = []
    gots = {}

    def zsend(d, k, h):
        slot = (slot_r if d == 0 else slot_l)(k)
        rows = rows_of(slot, h)
        r = remote(A.at[slot, h, rows], V.at[d, k - 1, h, rows], zs.at[d, k - 1, h], zr.at[d, k - 1, h], left if d == 0 else right)
        r.start()
        sends.append(r)
        gots[d, k - 1, h] = r

    def msend(d, k):
        slot = (slot_r if d == 0 else slot_l)(k)
        r = remote(GA.at[slot], GV.at[d, k - 1], ms.at[d, k - 1], mr.at[d, k - 1], left if d == 0 else right)
        r.start()
        sends.append(r)
        gots[d, k - 1, 2] = r

    def add(slot, h, more, dst):
        @pl.loop(0, TOK, step=32)
        def _(at):
            rows = pl.ds(pl.multiple_of(at, 32), 32)
            total = A[slot, h, rows].astype(F32)
            for d, k in more:
                total += V[d, k, h, rows].astype(F32)
            dst[rows] = total.astype(BF)

    def add_gate(slot, more):
        total = GA[slot].astype(F32)
        for d, k in more:
            total += GV[d, k].astype(F32)
        return total.astype(BF)

    def choose(p):
        slots = pair_slots(p)
        hot, weight, eqs = selection(M[slots[0]], M[slots[1]], z * 8, c)
        gate = jnp.sum(weight, axis=1, keepdims=True)
        return (routes(slots, 0, weight, c, gate), routes(slots, 1, hot, c)), eqs

    def unpack(p, chosen):
        slots = pair_slots(p)
        ways, eqs = chosen
        rows = pl.ds(p * 16, 16)
        over = (((0,), (0,)), ((), ()))
        for n, w in enumerate(ways):
            v = jnp.concatenate([b[n, q, rows] for b in (OB, OR) for q in range(NY)], axis=0)
            u = lax.dot_general(w, v, over, preferred_element_type=F32).astype(BF)
            for h, slot in enumerate(slots):
                A[slot, n] = u[h * TOK : (h + 1) * TOK]
        dots = jnp.concatenate([b[q, rows] for b in (SB, SR) for q in range(NY)], axis=0)
        for h, slot in enumerate(slots):
            gp = [jnp.sum(jnp.where(eq, dots, 0.0), axis=0, keepdims=True) for eq in eqs[h]]
            GA[slot] = jnp.concatenate(gp + [jnp.zeros((12, TOK), F32)], axis=0).astype(BF)

    near.wait()
    chosen, second = choose(0), choose(7)
    for r in core:
        r.wait_recv()
    unpack(0, chosen)
    for k in range(8, 0, -1):
        order = [(0, 1), (1, 0), (0, 0), (1, 1)] if k == 7 else [(0, 0), (1, 1)] if k == 8 else [(0, 0), (1, 0), (0, 1), (1, 1)]
        for d, h in order:
            slot = (slot_r if d == 0 else slot_l)(k)
            if (d, k, h) in gots:
                gots[d, k, h].wait_recv()
                came = PACKED.get(((slot_r if d == 0 else slot_l)(k + 1), h))
                if came is None:
                    add(slot, h, [(d, k)], A.at[slot, h])
                elif came == 8:
                    total = A[slot, h, 32:80].astype(F32) + V[d, k, h, 0:48].astype(F32)
                    A[slot, h, 32:80] = total.astype(BF)
                else:
                    total = lax.dot_general(hots[d], V[d, k, h, 0:80], (((0,), (0,)), ((), ())), preferred_element_type=F32)
                    A[slot, h] = (total + A[slot, h].astype(F32)).astype(BF)
            zsend(d, k, h)
        for d in (0, 1) if k < 8 else (0,):
            slot = (slot_r if d == 0 else slot_l)(k)
            if (d, k, 2) in gots:
                gots[d, k, 2].wait_recv()
                GA[slot] = add_gate(slot, [(d, k)])
            msend(d, k)
        if k > 1:
            unpack(k - 1, second if k == 8 else choose(k - 1))
        hots = [ahead(M[2 * k - 3 + d], z, d) if k in (7, 6) else None for d in (0, 1)]
        if k in (7, 6):
            weigh(2 * (7 - k))
            weigh(2 * (7 - k) + 1)
        if k == 6:
            for r in w1 + wl:
                r.start()
        if k == 2:
            for r in wl:
                r.wait()
            for r in w1:
                r.wait_recv()

            @pl.loop(0, D, step=32)
            def _(at):
                rows = pl.ds(pl.multiple_of(at, 32), 32)
                total = PU[y, rows].astype(F32)
                for i in range(3):
                    total += RU[i, rows].astype(F32)
                SU[rows] = total.astype(BF)

            @pl.loop(0, NY)
            def _(j):
                @pl.loop(0, FF, step=64)
                def _(at):
                    rows = pl.ds(pl.multiple_of(at, 64), 64)
                    total = OD[j, rows].astype(F32)
                    for i in range(3):
                        total += RD[i, j, rows].astype(F32)
                    SD[j, rows] = total.astype(BF)

            w2 = [remote(SU.at[xcols[i + 1]], RU2.at[i], ws.at[6 + i], wr.at[6 + i], xs[i]) for i in range(3)]
            w2 += [remote(SD.at[yat[i + 1]], RD2.at[i], ws.at[9 + i], wr.at[9 + i], ys[i]) for i in range(3)]
            for r in w2:
                r.start()
        if k == 1:
            for r in w2:
                r.wait_recv()

            @pl.loop(0, 256, step=32)
            def _(at):
                rows = pl.ds(pl.multiple_of(at, 32), 32)
                total = SU[pl.ds(pl.multiple_of(x * 256 + at, 32), 32)].astype(F32)
                for i in range(3):
                    total += RU2[i, rows].astype(F32)
                SU2[rows] = total.astype(BF)

            @pl.loop(0, FF, step=64)
            def _(at):
                rows = pl.ds(pl.multiple_of(at, 64), 64)
                total = SD[y, rows].astype(F32)
                for i in range(3):
                    total += RD2[i, rows].astype(F32)
                SD2[rows] = total.astype(BF)

            theirs = pl.ds(pl.multiple_of((1 - c) * 128, 128), 128)
            w3 = [
                remote(SU2.at[theirs], RU3, ws.at[12], wr.at[12], sib),
                remote(SD2.at[:, theirs], RD3, ws.at[13], wr.at[13], sib),
            ]
            for r in w3:
                r.start()
    for r in w3:
        r.wait_recv()
    mine = pl.ds(pl.multiple_of(c * 128, 128), 128)
    last = [
        pltpu.make_async_copy(SU2.at[mine], UG.at[c], loc.at[9]),
        pltpu.make_async_copy(RU3, UG.at[1 - c], loc.at[10]),
        pltpu.make_async_copy(SD2.at[:, mine], DG.at[c], loc.at[11]),
        pltpu.make_async_copy(RD3, DG.at[1 - c], loc.at[12]),
    ]
    for r in last:
        r.start()
    for h in (0, 1):
        for d in (0, 1):
            gots[d, 0, h].wait_recv()
        add(0, h, [(0, 0), (1, 0)], FV.at[h])
        r = pltpu.make_async_copy(FV.at[h], F.at[h], loc.at[13 + h])
        r.start()
        last.append(r)
    for d in (0, 1):
        gots[d, 0, 2].wait_recv()
    GF[...] = add_gate(0, [(0, 0), (1, 0)])
    r = pltpu.make_async_copy(GF, GO, loc.at[15])
    r.start()
    last.append(r)
    for r in sends + w1 + w2 + w3 + core:
        r.wait_send()
    for r in last:
        r.wait()


def out_kernel(F, G, UG, DG, mixed, back, gate, upg, dng):
    mixed[...] = F[0]
    back[...] = F[1]
    gate[...] = G[0:TOP]
    upg[...] = UG[...].astype(F32)
    dng[...] = DG[...].astype(F32)


def shards(tokens, expert_ids, gates, w_up, w_down, out_grad):
    dma = pltpu.SemaphoreType.DMA
    sd = jax.ShapeDtypeStruct
    vm = pltpu.VMEM
    X, M, WU, WD = pl.pallas_call(
        ag_kernel,
        name="gather",
        out_shape=(
            sd((3, NY, 256, D), BF),
            sd((NZ, 16, TOK), BF),
            sd((NY, D, FF), BF),
            sd((NY, FF, D), BF),
        ),
        in_specs=[ANY, ANY, VM, VM, ANY, ANY],
        out_specs=[ANY] * 4,
        scratch_shapes=[vm((NZ, 2, TOK, D), BF), vm((NZ, 16, TOK), BF), vm((8, 2, 3, NY, 16, D), BF), vm((4, 80, D), BF)]
        + [dma((2, 8, 2))] * 2 + [dma((2, 8))] * 2 + [dma((8,))] * 3 + [dma((14,))] * 2 + [dma((5,))],
        compiler_params=pltpu.CompilerParams(collective_id=1, has_side_effects=True, vmem_limit_bytes=60 << 20),
    )(tokens, out_grad, expert_ids.T, gates.T, w_up, w_down)

    parts = pl.pallas_call(
        rs_kernel,
        name="scatter",
        out_shape=(
            sd((2, TOK, D), BF),
            sd((16, TOK), BF),
            sd((2, D // 8, FF), BF),
            sd((2, FF, D // 8), BF),
        ),
        in_specs=[ANY] * 4,
        out_specs=[ANY] * 4,
        scratch_shapes=[
            vm((3, NY, 256, D), BF), vm((2, D, FF), BF), vm((2, FF, D), BF),
            vm((2, NY, 256, D), BF), vm((2, NY, 128, D), BF), vm((NY, 256, 128), F32), vm((NY, 128, 128), F32),
            vm((NY, 256, FF), BF), vm((NY, 256, FF), BF), vm((NY, D, FF), BF), vm((NY, FF, D), BF),
            vm((NZ, 16, TOK), BF), vm((NZ, 2, TOK, D), BF), vm((2, 8, 2, TOK, D), BF),
            vm((NZ, 16, TOK), BF), vm((2, 8, 16, TOK), BF), vm((2, TOK, D), BF), vm((16, TOK), BF),
            vm((3, D, FF), BF), vm((D, FF), BF), vm((3, 256, FF), BF), vm((256, FF), BF), vm((128, FF), BF),
            vm((3, NY, FF, 256), BF), vm((NY, FF, 256), BF), vm((NY, FF, 256), BF), vm((3, FF, 256), BF), vm((FF, 256), BF), vm((FF, 128), BF),
        ] + [dma((2, 8, 2))] * 2 + [dma((2, 8))] * 2 + [dma((8,))] * 2 + [dma((14,))] * 2 + [dma((16,)), dma((NY, 3))],
        compiler_params=pltpu.CompilerParams(collective_id=2, has_side_effects=True, vmem_limit_bytes=60 << 20),
    )(X, M, WU, WD)

    mixed, back, gate, upg, dng = pl.pallas_call(
        out_kernel,
        name="outputs",
        out_shape=(
            sd((TOK, D), BF),
            sd((TOK, D), BF),
            sd((TOP, TOK), BF),
            sd((2, D // 8, FF), F32),
            sd((2, FF, D // 8), F32),
        ),
        in_specs=[VM] * 4,
        out_specs=[VM] * 5,
    )(*parts)
    return mixed, back, gate.T, upg, dng


def solution(mesh):
    rows = P(("dp", "expert"), None)
    up, down = P("expert", "dp", None), P("expert", None, "dp")
    return jax.shard_map(
        shards,
        mesh=mesh,
        in_specs=(rows, rows, rows, up, down, rows),
        out_specs=(rows, rows, rows, up, down),
        check_vma=False,
    )
```
